512 devices in a mesh: tm: 64 (over y_lo, z, core), head: 8 (over y_hi, x).
Axes of the slice: x: 4, y: 8 (y_hi: 2, y_lo: 4; y = y_hi * 4 + y_lo), z: 8, core: 2. Of those that a mesh axis runs over, the one named last changes fastest.
Arguments:
- queries: bfloat16 [32768, 2048], P('tm', 'head'), may hold values from -12 to 12
- keys: bfloat16 [32768, 2048], P('tm', 'head'), may hold values from -6 to 6
- values: bfloat16 [32768, 2048], P('tm', 'head'), may hold values from -6 to 6
- outputs: bfloat16 [32768, 2048], P('tm', 'head'), may hold values from -4 to 4
- out_cotangent: bfloat16 [32768, 2048], P('tm', 'head'), may hold values from -256 to 256
- out_weight: bfloat16 [2048, 2048], P(None, 'head'), may hold values from -0.125 to 0.125
- block_pick: int32 [64, 5], P('tm'), may hold values from 0 to 1
Outputs:
- query_grad: bfloat16 [32768, 2048], P('tm', 'head')
- key_grad: bfloat16 [32768, 2048], P('tm', 'head')
- value_grad: bfloat16 [32768, 2048], P('tm', 'head')
- weight_grad: float32 [2048, 2048], P('tm', 'head')
The draws below stay inside these ranges and needn't reach their ends.
All inputs are finite; a program needn't handle non-finite values.
Results may differ from the reference program's by a relative error of at most 0.02.
Values may be sent and summed in bfloat16 or wider, within the bound.
No kernel may reach another device: no remote copies, remote signals or barrier semaphores. Data moves between devices by JAX's collectives and lax.ppermute only.
A program may use at most 64 MiB of HBM per device.

```python
import jax
import jax.numpy as jnp
from jax import lax

D = 2048
HEADS = 16
HD = 128
TOK_DEV = 512
WIN = 256
BLK = 128
LEVELS = 5
TOKENS = 32768
N_TM = 64


def draw_queries(key, part):
    key = jax.random.fold_in(key, 5)
    result = jnp.clip(jax.random.normal(key, (TOKENS, HEADS * HD), jnp.float32), -6.0, 6.0)
    return result.astype(jnp.bfloat16)


def draw_keys(key, part):
    key = jax.random.fold_in(key, 3)
    result = jnp.clip(jax.random.normal(key, (TOKENS, HEADS * HD), jnp.float32), -6.0, 6.0)
    return result.astype(jnp.bfloat16)


def touch_ends(values, stream_key, low, high):
    longest = values.shape.index(max(values.shape))
    spots = []
    for shift in (0, 1):
        where = [jax.random.randint(jax.random.fold_in(stream_key, axis), (), 0, length) for axis, length in enumerate(values.shape)]
        where[longest] = (where[longest] + shift) % values.shape[longest]
        spots.append(tuple(where))
    return values.at[spots[0]].set(low).at[spots[1]].set(high)


def raised(values, rng, source, target, blocks, factor):
    def block_of(axis_at):
        return (jnp.arange(values.shape[axis_at]) // (values.shape[axis_at] // blocks)).reshape((-1,) + (1,) * (values.ndim - 1 - axis_at))

    first = jax.random.permutation(rng, blocks)[block_of(target)]
    other_side = (block_of(target) + blocks // 2) % blocks
    return jnp.where((block_of(source) == first) | (block_of(source) == other_side), factor * values, values)


def level_of(stream_key, dims, shards, smallest, largest):
    level = 1.0
    for dim, blocks in shards:
        heights = jax.random.uniform(jax.random.fold_in(jax.random.fold_in(stream_key, 6), dim), (blocks,), jnp.float32, smallest / len(shards), largest / len(shards))
        level = level * jnp.repeat(jnp.exp(heights), dims[dim] // blocks).reshape((-1,) + (1,) * (len(dims) - 1 - dim))
    return level


def scatter_about(stream_key, extent, scale, reach, shards=(), held_as=jnp.bfloat16):
    drawn = jax.random.normal(stream_key, extent, jnp.float32) * scale
    if len(shards) > 0:
        drawn = level_of(stream_key, extent, shards, -0.22, 0.18) * drawn
    return jnp.clip(drawn, min=-reach, max=reach).astype(held_as)


def heavy_noise(own_key, dims, deviation, reach, pieces, heavy, kind=jnp.bfloat16):
    values = deviation * jax.random.normal(own_key, dims, jnp.float32)
    if pieces:
        values = values * level_of(own_key, dims, pieces, -0.22, 0.18)
    return jnp.clip(raised(values, jax.random.fold_in(own_key, 3), *heavy), -reach, reach).astype(kind)


def setup_inputs(seed: int = 0) -> dict:
    key_of = jax.random.split(jax.random.key(seed), 8)
    return {
        "queries": draw_queries(jax.random.fold_in(key_of[7], 71), 0),
        "keys": draw_keys(jax.random.fold_in(key_of[7], 71), 0),
        "values": scatter_about(key_of[2], (TOKENS, HEADS * HD), 1.0, 6.0, ((0, 64), (1, 8))),
        "outputs": scatter_about(key_of[3], (TOKENS, HEADS * HD), 0.25, 4.0, ((0, 64), (1, 8))),
        "out_cotangent": heavy_noise(key_of[4], (TOKENS, D), 16.0, 256.0, ((0, 64), (1, 8)), (0, 1, 64, 4.0)),
        "out_weight": scatter_about(key_of[5], (D, HEADS * HD), (HEADS * HD) ** -0.5, 0.125, ((1, 8),)),
        "block_pick": touch_ends(jax.random.randint(key_of[6], (N_TM, LEVELS), 0, (TOK_DEV - WIN) // BLK), jax.random.fold_in(key_of[6], 1), 0, ((TOK_DEV - WIN) // BLK) - 1).astype(jnp.int32),
    }


def head_grads(head_q, head_k, head_v, head_do, head_delta, block_pick):
    scale = HD ** -0.5

    def step(t, carry):
        grad_q, grad_k, grad_v = carry
        near = t * TOK_DEV - WIN + jnp.arange(WIN + TOK_DEV, dtype=jnp.int32)
        near_ok = near >= 0
        far_list = []
        far_ok = []
        for level in range(LEVELS):
            source = t - 2 ** level
            pick = block_pick[jnp.maximum(source, 0), level]
            far_list.append(source * TOK_DEV + pick * BLK + jnp.arange(BLK, dtype=jnp.int32))
            far_ok.append(jnp.full((BLK,), source >= 0))
        index = jnp.concatenate([near] + far_list).astype(jnp.int32)
        is_near = jnp.concatenate([jnp.ones((WIN + TOK_DEV,), bool), jnp.zeros((LEVELS * BLK,), bool)])
        valid = jnp.concatenate([near_ok] + far_ok)
        clipped = jnp.clip(index, 0, TOKENS - 1).astype(jnp.int32)
        key_rows = head_k[clipped]
        value_rows = head_v[clipped]
        start = (t * TOK_DEV).astype(jnp.int32)
        q_rows = lax.dynamic_slice_in_dim(head_q, start, TOK_DEV, 0)
        do_rows = lax.dynamic_slice_in_dim(head_do, start, TOK_DEV, 0)
        delta_rows = lax.dynamic_slice_in_dim(head_delta, start, TOK_DEV, 0)
        qpos = start + jnp.arange(TOK_DEV, dtype=jnp.int32)
        dist = qpos[:, None] - index[None, :]
        window_ok = (dist >= 0) & (dist < WIN)
        mask = valid[None, :] & jnp.where(is_near[None, :], window_ok, True)
        scores = jnp.dot(q_rows, key_rows.T, preferred_element_type=jnp.float32) * scale
        masked = jnp.where(mask, scores, jnp.float32(-1e30))
        top = jnp.max(masked, axis=1)
        lse = top + jnp.log(jnp.sum(jnp.exp(masked - top[:, None]), axis=1))
        probs = jnp.exp(masked - lse[:, None])
        probs_b = probs.astype(jnp.bfloat16)
        dprobs = jnp.dot(do_rows, value_rows.T, preferred_element_type=jnp.float32)
        dscores = (probs * (dprobs - delta_rows[:, None])).astype(jnp.bfloat16)
        dq_rows = jnp.dot(dscores, key_rows, preferred_element_type=jnp.float32) * scale
        dk_rows = jnp.dot(dscores.T, q_rows, preferred_element_type=jnp.float32) * scale
        dv_rows = jnp.dot(probs_b.T, do_rows, preferred_element_type=jnp.float32)
        keep = valid[:, None]
        grad_q = lax.dynamic_update_slice_in_dim(grad_q, dq_rows, start, 0)
        grad_k = grad_k.at[clipped].add(jnp.where(keep, dk_rows, jnp.float32(0.0)))
        grad_v = grad_v.at[clipped].add(jnp.where(keep, dv_rows, jnp.float32(0.0)))
        return grad_q, grad_k, grad_v

    zeros = jnp.zeros((TOKENS, HD), jnp.float32)
    grad_q, grad_k, grad_v = lax.fori_loop(0, N_TM, step, (zeros, zeros, zeros))
    return grad_q.astype(jnp.bfloat16), grad_k.astype(jnp.bfloat16), grad_v.astype(jnp.bfloat16)


def reference(queries, keys, values, outputs, out_cotangent, out_weight, block_pick):
    d_out = jnp.dot(out_cotangent, out_weight, preferred_element_type=jnp.float32).astype(jnp.bfloat16)
    weight_grad = lax.dot_general(out_cotangent, outputs, (((0,), (0,)), ((), ())), preferred_element_type=jnp.float32) * (TOKENS ** -0.5)
    delta = jnp.sum((d_out.astype(jnp.float32) * outputs.astype(jnp.float32)).reshape(TOKENS, HEADS, HD), axis=2)

    def split(array):
        return array.reshape(TOKENS, HEADS, HD).transpose(1, 0, 2)

    def one_head(packed):
        head_q, head_k, head_v, head_do, head_delta = packed
        return head_grads(head_q, head_k, head_v, head_do, head_delta, block_pick)

    grad_q, grad_k, grad_v = lax.map(one_head, (split(queries), split(keys), split(values), split(d_out), delta.T))

    def merge_heads(array):
        return array.transpose(1, 0, 2).reshape(TOKENS, HEADS * HD)

    return merge_heads(grad_q), merge_heads(grad_k), merge_heads(grad_v), weight_grad
```

```python
import functools

import jax
import jax.numpy as jnp
from jax import lax
from jax.experimental import pallas as pl
from jax.experimental.pallas import tpu as pltpu
from jax.sharding import PartitionSpec as P

HD = 128
WIN = 256
BLK = 128
LEVELS = 5
BF = jnp.bfloat16
F32 = jnp.float32
NX, NZ, NYL = 4, 8, 4
VMEM = pl.BlockSpec(memory_space=pltpu.VMEM)
SMEM = pl.BlockSpec(memory_space=pltpu.SMEM)


def params():
    return pltpu.CompilerParams(vmem_limit_bytes=40 * 1024 * 1024)


def dot(a, b, ca, cb):
    return lax.dot_general(a, b, (((ca,), (cb,)), ((), ())), preferred_element_type=F32)


def pack_kernel(info, k_ref, v_ref, near_ref, *far_refs):
    near_ref[0:WIN, :] = k_ref[512 - WIN :, :]
    near_ref[WIN : 2 * WIN, :] = v_ref[512 - WIN :, :]
    for level in range(LEVELS):
        first = pl.multiple_of(info[2 + level] * BLK, BLK)
        ref, at = (near_ref, 2 * WIN) if level == 0 else (far_refs[level - 1], 0)
        ref[at : at + BLK, :] = k_ref[pl.ds(first, BLK), :]
        ref[at + BLK : at + 2 * BLK, :] = v_ref[pl.ds(first, BLK), :]


def pack(info, keys, values):
    return pl.pallas_call(
        pack_kernel,
        out_shape=[jax.ShapeDtypeStruct((2 * WIN + 2 * BLK, 256), BF)]
        + [jax.ShapeDtypeStruct((2 * BLK, 256), BF)] * (LEVELS - 1),
        in_specs=[SMEM, VMEM, VMEM],
        out_specs=[VMEM] * LEVELS,
        compiler_params=params(),
        name="pack",
    )(info, keys, values)


def project_kernel(info, *refs):
    pieces = refs[:8]
    w_ref, o_ref, dout_ref, keep_ref, send_ref = refs[8:]
    core, head = info[0] % 2, info[1]
    yh, x = head // NX, head % NX
    o = o_ref[...]
    acc = jnp.zeros((512, 256), F32)
    for at in range(8):
        src = (yh ^ (at // NX)) * NX + (x + NX - at % NX) % NX
        cot = pieces[at][...]
        acc = acc + dot(cot, w_ref[pl.ds(pl.multiple_of(src * 256, 256), 256), :], 1, 0)
        term = dot(cot, o, 0, 0).astype(BF)
        yl, z0 = src // 2, (src % 2) * 4
        for sub in range(4):
            rows = pl.ds(pl.multiple_of((z0 + sub) * 128 + yl * 32, 32), 32)
            low = term[sub * 64 : sub * 64 + 32, :]
            high = term[sub * 64 + 32 : sub * 64 + 64, :]
            keep_ref[rows, :] = jnp.where(core == 0, low, high)
            send_ref[rows, :] = jnp.where(core == 0, high, low)
    dout_ref[...] = acc.astype(BF)


def project(info, pieces, out_weight, outputs):
    half = jax.ShapeDtypeStruct((1024, 256), BF)
    return pl.pallas_call(
        project_kernel,
        out_shape=[jax.ShapeDtypeStruct((512, 256), BF), half, half],
        in_specs=[SMEM] + [VMEM] * 10,
        out_specs=[VMEM] * 3,
        compiler_params=params(),
        name="project",
    )(info, *pieces, out_weight, outputs)


def attend_kernel(
    info, q_ref, k_ref, v_ref, o_ref, do_ref, near_ref, f1, f2, f3, f4,
    dq_ref, own_k, own_v, back_near, b1, b2, b3, b4,
    nk, nv, fk, fv,
):
    scale = HD ** (-0.5)
    shard = info[0]
    fars = (near_ref, f1, f2, f3, f4)
    neg = jnp.float32(-1e30)
    row = lax.broadcasted_iota(jnp.int32, (256, 256), 0)
    col = lax.broadcasted_iota(jnp.int32, (256, 256), 1)
    earlier = row > col
    level_of = lax.broadcasted_iota(jnp.int32, (LEVELS * BLK, 256), 0) // BLK
    far_ok = shard >= (1 << level_of)
    for head in range(2):
        lanes = slice(head * HD, (head + 1) * HD)
        k_far = jnp.concatenate(
            [r[(2 * WIN if i == 0 else 0) :, lanes][:BLK] for i, r in enumerate(fars)], axis=0
        )
        v_far = jnp.concatenate(
            [r[(2 * WIN if i == 0 else 0) + BLK :, lanes] for i, r in enumerate(fars)], axis=0
        )
        fk_acc = fv_acc = None
        mid = None
        for blk in range(2):
            rows = slice(blk * 256, (blk + 1) * 256)
            q = q_ref[rows, lanes]
            do = do_ref[rows, lanes]
            k_here, v_here = k_ref[rows, lanes], v_ref[rows, lanes]
            if blk == 0:
                k_prev, v_prev = near_ref[0:WIN, lanes], near_ref[WIN : 2 * WIN, lanes]
            else:
                k_prev, v_prev = k_ref[0:256, lanes], v_ref[0:256, lanes]
            delta = jnp.sum(
                do.astype(F32) * o_ref[rows, lanes].astype(F32), axis=1, keepdims=True
            )
            delta = jnp.transpose(jnp.broadcast_to(delta, (256, 128)))[0:1, :]
            s_prev = dot(k_prev, q, 1, 1)
            s_here = dot(k_here, q, 1, 1)
            s_far = dot(k_far, q, 1, 1)
            if blk == 0:
                s_prev = jnp.where(shard > 0, s_prev * scale, neg)
            else:
                s_prev = s_prev * scale
            s_near = jnp.where(earlier, s_prev, s_here * scale)
            s_far = jnp.where(far_ok, s_far * scale, neg)
            top = jnp.maximum(
                jnp.max(s_near, axis=0, keepdims=True), jnp.max(s_far, axis=0, keepdims=True)
            )
            e_near, e_far = jnp.exp(s_near - top), jnp.exp(s_far - top)
            inv = 1.0 / (
                jnp.sum(e_near, axis=0, keepdims=True) + jnp.sum(e_far, axis=0, keepdims=True)
            )
            p_near, p_far = e_near * inv, e_far * inv
            dp_near = jnp.where(earlier, dot(v_prev, do, 1, 1), dot(v_here, do, 1, 1))
            dp_far = dot(v_far, do, 1, 1)
            ds_near = p_near * (dp_near - delta)
            ds_far = (p_far * (dp_far - delta)).astype(BF)
            zero = jnp.zeros((), F32)
            ds_prev = jnp.where(earlier, ds_near, zero).astype(BF)
            ds_here = jnp.where(earlier, zero, ds_near).astype(BF)
            p_prev = jnp.where(earlier, p_near, zero).astype(BF)
            p_here = jnp.where(earlier, zero, p_near).astype(BF)
            p_far = p_far.astype(BF)
            dq = dot(ds_prev, k_prev, 0, 0) + dot(ds_here, k_here, 0, 0) + dot(ds_far, k_far, 0, 0)
            dq_ref[rows, lanes] = (dq * scale).astype(BF)
            dk_prev, dv_prev = dot(ds_prev, q, 1, 0) * scale, dot(p_prev, do, 1, 0)
            dk_here, dv_here = dot(ds_here, q, 1, 0) * scale, dot(p_here, do, 1, 0)
            dk_far, dv_far = dot(ds_far, q, 1, 0) * scale, dot(p_far, do, 1, 0)
            if blk == 0:
                back_near[0:WIN, lanes] = dk_prev.astype(BF)
                back_near[WIN : 2 * WIN, lanes] = dv_prev.astype(BF)
                own_k[0:256, lanes] = dk_here
                own_v[0:256, lanes] = dv_here
                fk[...] = dk_far
                fv[...] = dv_far
            else:
                own_k[0:256, lanes] += dk_prev
                own_v[0:256, lanes] += dv_prev
                own_k[256:512, lanes] = dk_here
                own_v[256:512, lanes] = dv_here
                for i, r in enumerate((back_near, b1, b2, b3, b4)):
                    at = 2 * WIN if i == 0 else 0
                    part = slice(i * BLK, (i + 1) * BLK)
                    r[at : at + BLK, lanes] = (fk[part, :] + dk_far[part]).astype(BF)
                    r[at + BLK : at + 2 * BLK, lanes] = (fv[part, :] + dv_far[part]).astype(BF)


def attend(info, queries, keys, values, outputs, d_out, got):
    f32s = jax.ShapeDtypeStruct((512, 256), F32)
    far = jax.ShapeDtypeStruct((2 * BLK, 256), BF)
    return pl.pallas_call(
        attend_kernel,
        out_shape=[
            jax.ShapeDtypeStruct((512, 256), BF), f32s, f32s,
            jax.ShapeDtypeStruct((2 * WIN + 2 * BLK, 256), BF), far, far, far, far,
        ],
        in_specs=[SMEM] + [VMEM] * 10,
        out_specs=[VMEM] * 8,
        scratch_shapes=[
            pltpu.VMEM((8, 128), F32), pltpu.VMEM((8, 128), F32),
            pltpu.VMEM((LEVELS * BLK, HD), F32), pltpu.VMEM((LEVELS * BLK, HD), F32),
        ],
        compiler_params=params(),
        name="attend",
    )(info, queries, keys, values, outputs, d_out, *got)


def finish_kernel(info, own_k, own_v, near_ref, f1, f2, f3, f4, dk_ref, dv_ref, tk, tv):
    for ref, acc, at in ((own_k, tk, 0), (own_v, tv, 1)):
        acc[0:256, :] = ref[0:256, :]
        acc[256:512, :] = ref[256:512, :] + near_ref[at * WIN : (at + 1) * WIN, :].astype(F32)
        for level, far in enumerate((near_ref, f1, f2, f3, f4)):
            low = (2 * WIN if level == 0 else 0) + at * BLK
            rows = pl.ds(pl.multiple_of(info[2 + level] * BLK, BLK), BLK)
            acc[rows, :] += far[low : low + BLK, :].astype(F32)
    dk_ref[...] = tk[...].astype(BF)
    dv_ref[...] = tv[...].astype(BF)


def finish(info, own_k, own_v, got):
    out = jax.ShapeDtypeStruct((512, 256), BF)
    return pl.pallas_call(
        finish_kernel,
        out_shape=[out, out],
        in_specs=[SMEM] + [VMEM] * 7,
        out_specs=[VMEM] * 2,
        scratch_shapes=[pltpu.VMEM((512, 256), F32)] * 2,
        compiler_params=params(),
        name="finish",
    )(info, own_k, own_v, *got)


def shift(block, distance):
    return lax.ppermute(
        block, "tm", [(i, i + distance) for i in range(64) if 0 <= i + distance < 64]
    )


def turn_x(block, offset):
    return lax.ppermute(
        block, "head", [(h, h // NX * NX + (h % NX + offset) % NX) for h in range(2 * NX)]
    )


def on_device(queries, keys, values, outputs, out_cotangent, out_weight, block_pick):
    shard = lax.axis_index("tm")
    info = jnp.concatenate(
        [
            shard.astype(jnp.int32)[None],
            lax.axis_index("head").astype(jnp.int32)[None],
            block_pick[0],
        ]
    )
    other = lax.ppermute(out_cotangent, "head", [(h, (h + NX) % (2 * NX)) for h in range(2 * NX)])
    mine = [out_cotangent] + [turn_x(out_cotangent, o) for o in range(1, NX)]
    packed = pack(info, keys, values)
    got = [shift(b, 2**level) for level, b in enumerate(packed)]
    theirs = [other] + [turn_x(other, o) for o in range(1, NX)]
    d_out, keep, send = project(info, mine + theirs, out_weight, outputs)
    received = lax.ppermute(send, "tm", [(i, i ^ 1) for i in range(64)])
    dq, own_k, own_v, *back = attend(info, queries, keys, values, outputs, d_out, got)
    back = [shift(b, -(2**level)) for level, b in enumerate(back)]
    half = (keep.astype(F32) + received.astype(F32)).astype(BF).reshape(NZ, NYL * 32, 256)
    z_groups = [[yl * 16 + z * 2 + c for z in range(NZ)] for yl in range(NYL) for c in range(2)]
    half = lax.all_to_all(half, "tm", 0, 0, axis_index_groups=z_groups)
    part = jnp.sum(half.astype(F32), axis=0).astype(BF).reshape(NYL, 32, 256)
    y_groups = [[yl * 16 + zc for yl in range(NYL)] for zc in range(16)]
    part = lax.all_to_all(part, "tm", 0, 0, axis_index_groups=y_groups)
    weight_grad = jnp.sum(part.astype(F32), axis=0) * (512 * 64) ** (-0.5)
    dk, dv = finish(info, own_k, own_v, back)
    return dq, dk, dv, weight_grad


def solution(mesh):
    placed = (P("tm", "head"),) * 5 + (P(None, "head"), P("tm", None))
    return jax.shard_map(
        on_device,
        mesh=mesh,
        in_specs=placed,
        out_specs=(P("tm", "head"),) * 4,
        check_vma=False,
    )
```

```python
import functools

import functools

import jax
import jax.numpy as jnp
from jax import lax
from jax.experimental import pallas as pl
from jax.experimental.pallas import tpu as pltpu
from jax.sharding import PartitionSpec as P

HD = 128
WIN = 256
BLK = 128
LEVELS = 5
BF = jnp.bfloat16
F32 = jnp.float32
NX, NZ, NYL = 4, 8, 4
VMEM = pl.BlockSpec(memory_space=pltpu.VMEM)
ANY = pl.BlockSpec(memory_space=pl.ANY)
PROJECT_MIB = 60
AFTER = slice(0, 3)
SMEM = pl.BlockSpec(memory_space=pltpu.SMEM)


def params(mib=16):
    return pltpu.CompilerParams(vmem_limit_bytes=mib * 1024 * 1024)


def dot(a, b, ca, cb):
    return lax.dot_general(a, b, (((ca,), (cb,)), ((), ())), preferred_element_type=F32)


def pack_kernel(pick, k_ref, v_ref, near_ref, *far_refs):
    near_ref[0:WIN, :] = k_ref[512 - WIN :, :]
    near_ref[WIN : 2 * WIN, :] = v_ref[512 - WIN :, :]
    for level in range(LEVELS):
        first = pl.multiple_of(pick[0, level] * BLK, BLK)
        ref, at = (near_ref, 2 * WIN) if level == 0 else (far_refs[level - 1], 0)
        ref[at : at + BLK, :] = k_ref[pl.ds(first, BLK), :]
        ref[at + BLK : at + 2 * BLK, :] = v_ref[pl.ds(first, BLK), :]


def pack(pick, keys, values):
    return pl.pallas_call(
        pack_kernel,
        out_shape=[jax.ShapeDtypeStruct((2 * WIN + 2 * BLK, 256), BF)]
        + [jax.ShapeDtypeStruct((2 * BLK, 256), BF)] * (LEVELS - 1),
        in_specs=[SMEM, VMEM, VMEM],
        out_specs=[VMEM] * LEVELS,
        compiler_params=params(),
        name="pack",
    )(pick, keys, values)


def spread_kernel(n, b_ref, *refs):
    block = b_ref[...]
    for i in range(NX):
        refs[n][i] = block


def spread(block, *after):
    n = len(after)
    return pl.pallas_call(
        functools.partial(spread_kernel, n),
        out_shape=jax.ShapeDtypeStruct((NX, 512, 256), BF),
        in_specs=[VMEM] + [ANY] * n,
        out_specs=VMEM,
        compiler_params=params(),
        name="spread",
    )(block, *after)


def k_rows(near_ref, fars, lanes):
    return jnp.concatenate(
        [near_ref[2 * WIN : 2 * WIN + BLK, lanes]] + [r[0:BLK, lanes] for r in fars], axis=0
    )


def v_rows(near_ref, fars, lanes):
    return jnp.concatenate(
        [near_ref[2 * WIN + BLK :, lanes]] + [r[BLK:, lanes] for r in fars], axis=0
    )


def earlier_tile():
    row = lax.broadcasted_iota(jnp.int32, (256, 256), 0)
    col = lax.broadcasted_iota(jnp.int32, (256, 256), 1)
    return row > col


def weigh_kernel(
    q_ref, k_ref, near_ref, f1, f2, f3, f4, p_ref,
):
    scale = HD ** (-0.5)
    shard = lax.axis_index("tm")
    neg = jnp.float32(-1e30)
    earlier = earlier_tile()
    level_of = lax.broadcasted_iota(jnp.int32, (LEVELS * BLK, 256), 0) // BLK
    far_ok = shard >= (1 << level_of)
    for head in range(2):
        lanes = slice(head * HD, (head + 1) * HD)
        k_far = k_rows(near_ref, (f1, f2, f3, f4), lanes)
        for blk in range(2):
            rows = slice(blk * 256, (blk + 1) * 256)
            q = q_ref[rows, lanes]
            k_here = k_ref[rows, lanes]
            k_prev = near_ref[0:WIN, lanes] if blk == 0 else k_ref[0:256, lanes]
            s_prev = dot(k_prev, q, 1, 1) * scale
            s_here = dot(k_here, q, 1, 1) * scale
            s_far = dot(k_far, q, 1, 1) * scale
            if blk == 0:
                s_prev = jnp.where(shard > 0, s_prev, neg)
            s_near = jnp.where(earlier, s_prev, s_here)
            s_far = jnp.where(far_ok, s_far, neg)
            top = jnp.maximum(
                jnp.max(s_near, axis=0, keepdims=True), jnp.max(s_far, axis=0, keepdims=True)
            )
            e_near, e_far = jnp.exp(s_near - top), jnp.exp(s_far - top)
            inv = 1.0 / (
                jnp.sum(e_near, axis=0, keepdims=True) + jnp.sum(e_far, axis=0, keepdims=True)
            )
            p_ref[2 * head + blk, 0:256, :] = (e_near * inv).astype(BF)
            p_ref[2 * head + blk, 256:, :] = (e_far * inv).astype(BF)


def weigh(queries, keys, got):
    return pl.pallas_call(
        weigh_kernel,
        out_shape=jax.ShapeDtypeStruct((4, 256 + LEVELS * BLK, 256), BF),
        in_specs=[VMEM] * 7,
        out_specs=VMEM,
        compiler_params=params(),
        name="weigh",
    )(queries, keys, *got)


def project_kernel(
    mine_hbm, theirs_hbm, w_hbm, o_hbm, probs, dout_ref, keep_ref, send_ref,
    w_ref, cot_ref, o_ref, w_sems, cot_sems, o_sem,
):
    core, head = lax.axis_index("tm") % 2, lax.axis_index("head")
    yh = head // NX
    load_o = pltpu.make_async_copy(o_hbm, o_ref, o_sem)
    load_o.start()
    loads = []
    for at in range(2 * NX):
        src = (yh if at < NX else 1 - yh) * NX + at % NX
        rows = pl.ds(pl.multiple_of(src * 256, 256), 256)
        cots = mine_hbm if at < NX else theirs_hbm
        pair = (
            pltpu.make_async_copy(cots.at[at % NX], cot_ref.at[at], cot_sems.at[at]),
            pltpu.make_async_copy(w_hbm.at[rows, :], w_ref.at[at], w_sems.at[at]),
        )
        for load in pair:
            load.start()
        loads.append(pair)
    load_o.wait()
    acc = jnp.zeros((512, 256), F32)
    for at in range(2 * NX):
        src = (yh if at < NX else 1 - yh) * NX + at % NX
        loads[at][0].wait()
        cot = cot_ref[at]
        term = dot(cot, o_ref[...], 0, 0).astype(BF)
        for sub in range(4):
            rows = pl.ds(pl.multiple_of(src * 128 + sub * 32, 32), 32)
            low = term[sub * 64 : sub * 64 + 32, :]
            high = term[sub * 64 + 32 : sub * 64 + 64, :]
            keep_ref[rows, :] = jnp.where(core == 0, low, high)
            send_ref[rows, :] = jnp.where(core == 0, high, low)
        loads[at][1].wait()
        acc = acc + dot(cot, w_ref[at], 1, 0)
    dout_ref[...] = acc.astype(BF)


def project(mine, theirs, out_weight, outputs, probs):
    half = jax.ShapeDtypeStruct((1024, 256), BF)
    return pl.pallas_call(
        project_kernel,
        out_shape=[jax.ShapeDtypeStruct((512, 256), BF), half, half],
        in_specs=[ANY] * 5,
        out_specs=[VMEM] * 3,
        scratch_shapes=[
            pltpu.VMEM((2 * NX, 256, 256), BF),
            pltpu.VMEM((2 * NX, 512, 256), BF),
            pltpu.VMEM((512, 256), BF),
            pltpu.SemaphoreType.DMA((2 * NX,)),
            pltpu.SemaphoreType.DMA((2 * NX,)),
            pltpu.SemaphoreType.DMA,
        ],
        compiler_params=params(PROJECT_MIB),
        name="project",
    )(mine, theirs, out_weight, outputs, probs)


def attend_kernel(
    p_ref, q_ref, k_ref, v_ref, o_ref, do_ref, near_ref, f1, f2, f3, f4,
    dq_ref, own_k, own_v, back_near, b1, b2, b3, b4, fk, fv,
):
    scale = HD ** (-0.5)
    earlier = earlier_tile()
    zero = jnp.zeros((), F32)
    for head in range(2):
        lanes = slice(head * HD, (head + 1) * HD)
        k_far = k_rows(near_ref, (f1, f2, f3, f4), lanes)
        v_far = v_rows(near_ref, (f1, f2, f3, f4), lanes)
        for blk in range(2):
            rows = slice(blk * 256, (blk + 1) * 256)
            q = q_ref[rows, lanes]
            do = do_ref[rows, lanes]
            k_here, v_here = k_ref[rows, lanes], v_ref[rows, lanes]
            if blk == 0:
                k_prev, v_prev = near_ref[0:WIN, lanes], near_ref[WIN : 2 * WIN, lanes]
            else:
                k_prev, v_prev = k_ref[0:256, lanes], v_ref[0:256, lanes]
            delta = jnp.sum(
                do.astype(F32) * o_ref[rows, lanes].astype(F32), axis=1, keepdims=True
            )
            delta = jnp.transpose(jnp.broadcast_to(delta, (256, 128)))[0:1, :]
            p_near = p_ref[2 * head + blk, 0:256, :].astype(F32)
            p_far = p_ref[2 * head + blk, 256:, :]
            dp_near = jnp.where(earlier, dot(v_prev, do, 1, 1), dot(v_here, do, 1, 1))
            dp_far = dot(v_far, do, 1, 1)
            ds_near = p_near * (dp_near - delta)
            ds_far = (p_far.astype(F32) * (dp_far - delta)).astype(BF)
            ds_prev = jnp.where(earlier, ds_near, zero).astype(BF)
            ds_here = jnp.where(earlier, zero, ds_near).astype(BF)
            p_prev = jnp.where(earlier, p_near, zero).astype(BF)
            p_here = jnp.where(earlier, zero, p_near).astype(BF)
            dq = dot(ds_prev, k_prev, 0, 0) + dot(ds_here, k_here, 0, 0) + dot(ds_far, k_far, 0, 0)
            dq_ref[rows, lanes] = (dq * scale).astype(BF)
            dk_prev, dv_prev = dot(ds_prev, q, 1, 0) * scale, dot(p_prev, do, 1, 0)
            dk_here, dv_here = dot(ds_here, q, 1, 0) * scale, dot(p_here, do, 1, 0)
            dk_far, dv_far = dot(ds_far, q, 1, 0) * scale, dot(p_far, do, 1, 0)
            if blk == 0:
                back_near[0:WIN, lanes] = dk_prev.astype(BF)
                back_near[WIN : 2 * WIN, lanes] = dv_prev.astype(BF)
                own_k[0:256, lanes] = dk_here
                own_v[0:256, lanes] = dv_here
                fk[...] = dk_far
                fv[...] = dv_far
            else:
                own_k[0:256, lanes] += dk_prev
                own_v[0:256, lanes] += dv_prev
                own_k[256:512, lanes] = dk_here
                own_v[256:512, lanes] = dv_here
                for i, r in enumerate((back_near, b1, b2, b3, b4)):
                    at = 2 * WIN if i == 0 else 0
                    part = slice(i * BLK, (i + 1) * BLK)
                    r[at : at + BLK, lanes] = (fk[part, :] + dk_far[part]).astype(BF)
                    r[at + BLK : at + 2 * BLK, lanes] = (fv[part, :] + dv_far[part]).astype(BF)


def attend(probs, queries, keys, values, outputs, d_out, got):
    f32s = jax.ShapeDtypeStruct((512, 256), F32)
    far = jax.ShapeDtypeStruct((2 * BLK, 256), BF)
    return pl.pallas_call(
        attend_kernel,
        out_shape=[
            jax.ShapeDtypeStruct((512, 256), BF), f32s, f32s,
            jax.ShapeDtypeStruct((2 * WIN + 2 * BLK, 256), BF), far, far, far, far,
        ],
        in_specs=[VMEM] * 11,
        out_specs=[VMEM] * 8,
        scratch_shapes=[pltpu.VMEM((LEVELS * BLK, HD), F32)] * 2,
        compiler_params=params(),
        name="attend",
    )(probs, queries, keys, values, outputs, d_out, *got)


def finish_kernel(pick, own_k, own_v, near_ref, f1, f2, f3, f4, dk_ref, dv_ref, tk, tv):
    for ref, acc, at in ((own_k, tk, 0), (own_v, tv, 1)):
        acc[0:256, :] = ref[0:256, :]
        acc[256:512, :] = ref[256:512, :] + near_ref[at * WIN : (at + 1) * WIN, :].astype(F32)
        for level, far in enumerate((near_ref, f1, f2, f3, f4)):
            low = (2 * WIN if level == 0 else 0) + at * BLK
            rows = pl.ds(pl.multiple_of(pick[0, level] * BLK, BLK), BLK)
            acc[rows, :] += far[low : low + BLK, :].astype(F32)
    dk_ref[...] = tk[...].astype(BF)
    dv_ref[...] = tv[...].astype(BF)


def finish(pick, own_k, own_v, got):
    out = jax.ShapeDtypeStruct((512, 256), BF)
    return pl.pallas_call(
        finish_kernel,
        out_shape=[out, out],
        in_specs=[SMEM] + [VMEM] * 7,
        out_specs=[VMEM] * 2,
        scratch_shapes=[pltpu.VMEM((512, 256), F32)] * 2,
        compiler_params=params(),
        name="finish",
    )(pick, own_k, own_v, *got)


def shift(block, distance):
    return lax.ppermute(
        block, "tm", [(i, i + distance) for i in range(64) if 0 <= i + distance < 64]
    )


def to_row(blocks):
    rows = [[yh * NX + x for x in range(NX)] for yh in range(2)]
    return lax.all_to_all(blocks, "head", 0, 0, axis_index_groups=rows)


def on_device(queries, keys, values, outputs, out_cotangent, out_weight, block_pick):
    mine = to_row(spread(out_cotangent))
    other = lax.ppermute(out_cotangent, "head", [(h, (h + NX) % (2 * NX)) for h in range(2 * NX)])
    packed = pack(block_pick, keys, values)
    got = [shift(b, 2**level) for level, b in enumerate(packed)]
    theirs = to_row(spread(other, *got[AFTER]))
    probs = weigh(queries, keys, got)
    d_out, keep, send = project(mine, theirs, out_weight, outputs, probs)
    received = lax.ppermute(send, "tm", [(i, i ^ 1) for i in range(64)])
    dq, own_k, own_v, *back = attend(probs, queries, keys, values, outputs, d_out, got)
    back = [shift(b, -(2**level)) for level, b in enumerate(back)]
    half = (keep.astype(F32) + received.astype(F32)).astype(BF).reshape(NYL * NZ, 32, 256)
    groups = [[2 * i + c for i in range(NYL * NZ)] for c in range(2)]
    part = lax.all_to_all(half, "tm", 0, 0, axis_index_groups=groups)
    weight_grad = jnp.sum(part.astype(F32), axis=0) * (512 * 64) ** (-0.5)
    dk, dv = finish(block_pick, own_k, own_v, back)
    return dq, dk, dv, weight_grad


def solution(mesh):
    placed = (P("tm", "head"),) * 5 + (P(None, "head"), P("tm", None))
    return jax.shard_map(
        on_device,
        mesh=mesh,
        in_specs=placed,
        out_specs=(P("tm", "head"),) * 4,
        check_vma=False,
    )
```

```python
import jax
import jax.numpy as jnp
from jax import lax
from jax.experimental import pallas as pl
from jax.experimental.pallas import tpu as pltpu
from jax.sharding import PartitionSpec as P

HD = 128
WIN = 256
BLK = 128
LEVELS = 5
GATE_MIB = 60
ATTEND_MIB = 60
BF = jnp.bfloat16
F32 = jnp.float32
NX, NZ, NYL = 4, 8, 4
VMEM = pl.BlockSpec(memory_space=pltpu.VMEM)
PIECES = 1
ANY = pl.BlockSpec(memory_space=pl.ANY)
SMEM = pl.BlockSpec(memory_space=pltpu.SMEM)


def params(mib=16):
    return pltpu.CompilerParams(vmem_limit_bytes=mib * 1024 * 1024)


def dot(a, b, ca, cb):
    return lax.dot_general(a, b, (((ca,), (cb,)), ((), ())), preferred_element_type=F32)


def pack_kernel(pick, k_ref, v_ref, near_ref, *far_refs):
    near_ref[0:WIN, :] = k_ref[512 - WIN :, :]
    near_ref[WIN : 2 * WIN, :] = v_ref[512 - WIN :, :]
    for level in range(LEVELS):
        first = pl.multiple_of(pick[0, level] * BLK, BLK)
        ref, at = (near_ref, 2 * WIN) if level == 0 else (far_refs[level - 1], 0)
        ref[at : at + BLK, :] = k_ref[pl.ds(first, BLK), :]
        ref[at + BLK : at + 2 * BLK, :] = v_ref[pl.ds(first, BLK), :]


def pack(pick, keys, values):
    return pl.pallas_call(
        pack_kernel,
        out_shape=[jax.ShapeDtypeStruct((2 * WIN + 2 * BLK, 256), BF)]
        + [jax.ShapeDtypeStruct((2 * BLK, 256), BF)] * (LEVELS - 1),
        in_specs=[SMEM, VMEM, VMEM],
        out_specs=[VMEM] * LEVELS,
        compiler_params=params(),
        name="pack",
    )(pick, keys, values)


def k_rows(near_ref, fars, lanes):
    return jnp.concatenate(
        [near_ref[2 * WIN : 2 * WIN + BLK, lanes]] + [r[0:BLK, lanes] for r in fars], axis=0
    )


def v_rows(near_ref, fars, lanes):
    return jnp.concatenate(
        [near_ref[2 * WIN + BLK :, lanes]] + [r[BLK:, lanes] for r in fars], axis=0
    )


def earlier_tile():
    row = lax.broadcasted_iota(jnp.int32, (256, 256), 0)
    col = lax.broadcasted_iota(jnp.int32, (256, 256), 1)
    return row > col


def sources():
    head = lax.axis_index("head")
    yh = head // NX
    return [(yh if at < NX else 1 - yh) * NX + at % NX for at in range(2 * NX)]


def piece(refs, at):
    low = at // NX * 512
    return refs[0][at % NX, low : low + 512, :]


def gate_kernel(*refs):
    refs[-1][...] = jnp.zeros((8, 128), F32)


def gate(*got):
    return pl.pallas_call(
        gate_kernel,
        out_shape=jax.ShapeDtypeStruct((8, 128), F32),
        in_specs=[ANY] * len(got),
        out_specs=VMEM,
        compiler_params=params(GATE_MIB),
        cost_estimate=pl.CostEstimate(
            flops=13000000000, bytes_accessed=2**20, transcendentals=0
        ),
        name="gate",
    )(*got)


def project_kernel(*refs):
    pieces, (w_ref, o_ref, ready) = refs[:PIECES], refs[PIECES : PIECES + 3]
    dout_ref, keep_ref, send_ref = refs[PIECES + 3 :]
    core = lax.axis_index("tm") % 2
    o = o_ref[...]
    acc = jnp.zeros((512, 256), F32)
    for at, src in enumerate(sources()):
        cot = piece(pieces, at)
        acc = acc + dot(cot, w_ref[pl.ds(pl.multiple_of(src * 256, 256), 256), :], 1, 0)
        term = dot(cot, o, 0, 0).astype(BF)
        for sub in range(4):
            rows = pl.ds(pl.multiple_of(src * 128 + sub * 32, 32), 32)
            low = term[sub * 64 : sub * 64 + 32, :]
            high = term[sub * 64 + 32 : sub * 64 + 64, :]
            keep_ref[rows, :] = jnp.where(core == 0, low, high)
            send_ref[rows, :] = jnp.where(core == 0, high, low)
    dout_ref[...] = acc.astype(BF)


def project(pieces, out_weight, outputs, ready):
    half = jax.ShapeDtypeStruct((1024, 256), BF)
    return pl.pallas_call(
        project_kernel,
        out_shape=[jax.ShapeDtypeStruct((512, 256), BF), half, half],
        in_specs=[VMEM] * (PIECES + 2) + [ANY],
        out_specs=[VMEM] * 3,
        compiler_params=params(),
        name="project",
    )(*pieces, out_weight, outputs, ready)


def attend_kernel(
    q_hbm, k_hbm, v_hbm, o_hbm, do_hbm, near_hbm, f1, f2, f3, f4,
    dq_ref, own_k, own_v, back_near, b1, b2, b3, b4, token,
    q_ref, k_ref, v_ref, o_ref, do_ref, near_ref, f_ref, fk, fv, sems,
):
    token[...] = jnp.zeros((8, 128), F32)
    pairs = [(q_hbm, q_ref), (k_hbm, k_ref), (near_hbm, near_ref)]
    pairs += [(f, f_ref.at[i]) for i, f in enumerate((f1, f2, f3, f4))]
    pairs += [(v_hbm, v_ref), (do_hbm, do_ref), (o_hbm, o_ref)]
    loads = [pltpu.make_async_copy(src, dst, sems.at[i]) for i, (src, dst) in enumerate(pairs)]
    for load in loads:
        load.start()
    scale = HD ** (-0.5)
    shard = lax.axis_index("tm")
    neg = jnp.float32(-1e30)
    zero = jnp.zeros((), F32)
    earlier = earlier_tile()
    level_of = lax.broadcasted_iota(jnp.int32, (LEVELS * BLK, 256), 0) // BLK
    far_ok = shard >= (1 << level_of)
    fars = [f_ref.at[i] for i in range(LEVELS - 1)]
    for load in loads[: LEVELS + 2]:
        load.wait()
    for head in range(2):
        lanes = slice(head * HD, (head + 1) * HD)
        k_far = k_rows(near_ref, fars, lanes)
        v_far = v_rows(near_ref, fars, lanes)
        for blk in range(2):
            rows = slice(blk * 256, (blk + 1) * 256)
            q = q_ref[rows, lanes]
            k_here = k_ref[rows, lanes]
            k_prev = near_ref[0:WIN, lanes] if blk == 0 else k_ref[0:256, lanes]
            s_prev = dot(k_prev, q, 1, 1) * scale
            s_here = dot(k_here, q, 1, 1) * scale
            s_far = dot(k_far, q, 1, 1) * scale
            if blk == 0:
                s_prev = jnp.where(shard > 0, s_prev, neg)
            s_near = jnp.where(earlier, s_prev, s_here)
            s_far = jnp.where(far_ok, s_far, neg)
            top = jnp.maximum(
                jnp.max(s_near, axis=0, keepdims=True), jnp.max(s_far, axis=0, keepdims=True)
            )
            e_near, e_far = jnp.exp(s_near - top), jnp.exp(s_far - top)
            inv = 1.0 / (
                jnp.sum(e_near, axis=0, keepdims=True) + jnp.sum(e_far, axis=0, keepdims=True)
            )
            p_near, p_far = e_near * inv, e_far * inv
            if head == 0 and blk == 0:
                for load in loads[LEVELS + 2 :]:
                    load.wait()
            do = do_ref[rows, lanes]
            v_here = v_ref[rows, lanes]
            v_prev = near_ref[WIN : 2 * WIN, lanes] if blk == 0 else v_ref[0:256, lanes]
            delta = jnp.sum(
                do.astype(F32) * o_ref[rows, lanes].astype(F32), axis=1, keepdims=True
            )
            delta = jnp.transpose(jnp.broadcast_to(delta, (256, 128)))[0:1, :]
            dp_near = jnp.where(earlier, dot(v_prev, do, 1, 1), dot(v_here, do, 1, 1))
            dp_far = dot(v_far, do, 1, 1)
            ds_near = p_near * (dp_near - delta)
            ds_far = (p_far * (dp_far - delta)).astype(BF)
            ds_prev = jnp.where(earlier, ds_near, zero).astype(BF)
            ds_here = jnp.where(earlier, zero, ds_near).astype(BF)
            p_prev = jnp.where(earlier, p_near, zero).astype(BF)
            p_here = jnp.where(earlier, zero, p_near).astype(BF)
            p_far = p_far.astype(BF)
            dq = dot(ds_prev, k_prev, 0, 0) + dot(ds_here, k_here, 0, 0) + dot(ds_far, k_far, 0, 0)
            dq_ref[rows, lanes] = (dq * scale).astype(BF)
            dk_prev, dv_prev = dot(ds_prev, q, 1, 0) * scale, dot(p_prev, do, 1, 0)
            dk_here, dv_here = dot(ds_here, q, 1, 0) * scale, dot(p_here, do, 1, 0)
            dk_far, dv_far = dot(ds_far, q, 1, 0) * scale, dot(p_far, do, 1, 0)
            if blk == 0:
                back_near[0:WIN, lanes] = dk_prev.astype(BF)
                back_near[WIN : 2 * WIN, lanes] = dv_prev.astype(BF)
                own_k[0:256, lanes] = dk_here
                own_v[0:256, lanes] = dv_here
                fk[...] = dk_far
                fv[...] = dv_far
            else:
                own_k[0:256, lanes] += dk_prev
                own_v[0:256, lanes] += dv_prev
                own_k[256:512, lanes] = dk_here
                own_v[256:512, lanes] = dv_here
                for i, r in enumerate((back_near, b1, b2, b3, b4)):
                    at = 2 * WIN if i == 0 else 0
                    part = slice(i * BLK, (i + 1) * BLK)
                    r[at : at + BLK, lanes] = (fk[part, :] + dk_far[part]).astype(BF)
                    r[at + BLK : at + 2 * BLK, lanes] = (fv[part, :] + dv_far[part]).astype(BF)


def attend(queries, keys, values, outputs, d_out, got):
    f32s = jax.ShapeDtypeStruct((512, 256), F32)
    far = jax.ShapeDtypeStruct((2 * BLK, 256), BF)
    here = pltpu.VMEM((512, 256), BF)
    return pl.pallas_call(
        attend_kernel,
        out_shape=[
            jax.ShapeDtypeStruct((512, 256), BF), f32s, f32s,
            jax.ShapeDtypeStruct((2 * WIN + 2 * BLK, 256), BF), far, far, far, far,
            jax.ShapeDtypeStruct((8, 128), F32),
        ],
        in_specs=[ANY] * 10,
        out_specs=[VMEM] * 9,
        scratch_shapes=[
            here, here, here, here, here,
            pltpu.VMEM((2 * WIN + 2 * BLK, 256), BF),
            pltpu.VMEM((LEVELS - 1, 2 * BLK, 256), BF),
            pltpu.VMEM((LEVELS * BLK, HD), F32),
            pltpu.VMEM((LEVELS * BLK, HD), F32),
            pltpu.SemaphoreType.DMA((10,)),
        ],
        compiler_params=params(ATTEND_MIB),
        name="attend",
    )(queries, keys, values, outputs, d_out, *got)


def add_kernel(keep_ref, got_ref, out_ref):
    out_ref[...] = (keep_ref[...].astype(F32) + got_ref[...].astype(F32)).astype(BF)


def add(keep, received):
    return pl.pallas_call(
        add_kernel,
        out_shape=jax.ShapeDtypeStruct((1024, 256), BF),
        in_specs=[VMEM, VMEM],
        out_specs=VMEM,
        compiler_params=params(),
        name="add",
    )(keep, received)


def total_kernel(part_ref, out_ref):
    out_ref[...] = jnp.sum(part_ref[...].astype(F32), axis=0) * (512 * 64) ** (-0.5)


def total(part):
    return pl.pallas_call(
        total_kernel,
        out_shape=jax.ShapeDtypeStruct((32, 256), F32),
        in_specs=[VMEM],
        out_specs=VMEM,
        compiler_params=params(),
        name="total",
    )(part)


def finish_kernel(pick, own_k, own_v, near_ref, f1, f2, f3, f4, dk_ref, dv_ref, tk, tv):
    for ref, acc, at in ((own_k, tk, 0), (own_v, tv, 1)):
        acc[0:256, :] = ref[0:256, :]
        acc[256:512, :] = ref[256:512, :] + near_ref[at * WIN : (at + 1) * WIN, :].astype(F32)
        for level, far in enumerate((near_ref, f1, f2, f3, f4)):
            low = (2 * WIN if level == 0 else 0) + at * BLK
            rows = pl.ds(pl.multiple_of(pick[0, level] * BLK, BLK), BLK)
            acc[rows, :] += far[low : low + BLK, :].astype(F32)
    dk_ref[...] = tk[...].astype(BF)
    dv_ref[...] = tv[...].astype(BF)


def finish(pick, own_k, own_v, got):
    out = jax.ShapeDtypeStruct((512, 256), BF)
    return pl.pallas_call(
        finish_kernel,
        out_shape=[out, out],
        in_specs=[SMEM] + [VMEM] * 7,
        out_specs=[VMEM] * 2,
        scratch_shapes=[pltpu.VMEM((512, 256), F32)] * 2,
        compiler_params=params(),
        cost_estimate=pl.CostEstimate(
            flops=5000000000, bytes_accessed=2**20, transcendentals=0
        ),
        name="finish",
    )(pick, own_k, own_v, *got)


def shift(block, distance):
    return lax.ppermute(
        block, "tm", [(i, i + distance) for i in range(64) if 0 <= i + distance < 64]
    )


def spread_kernel(a_ref, b_ref, out_ref):
    for i in range(NX):
        out_ref[i, 0:512, :] = a_ref[...]
        out_ref[i, 512:1024, :] = b_ref[...]


def spread(block, other):
    return pl.pallas_call(
        spread_kernel,
        out_shape=jax.ShapeDtypeStruct((NX, 1024, 256), BF),
        in_specs=[VMEM] * 2,
        out_specs=VMEM,
        compiler_params=params(),
        name="spread",
    )(block, other)


def to_row(blocks):
    rows = [[yh * NX + x for x in range(NX)] for yh in range(2)]
    return lax.all_to_all(blocks, "head", 0, 0, axis_index_groups=rows)


def on_device(queries, keys, values, outputs, out_cotangent, out_weight, block_pick):
    other = lax.ppermute(out_cotangent, "head", [(h, (h + NX) % (2 * NX)) for h in range(2 * NX)])
    packed = pack(block_pick, keys, values)
    got = [shift(b, 2**level) for level, b in enumerate(packed)]
    pieces = [to_row(spread(out_cotangent, other))]
    ready = gate(got[0], got[1], got[2], got[3], got[4])
    d_out, keep, send = project(pieces, out_weight, outputs, ready)
    received = lax.ppermute(send, "tm", [(i, i ^ 1) for i in range(64)])
    dq, own_k, own_v, *back, token = attend(queries, keys, values, outputs, d_out, got)
    back = [shift(b, -(2**level)) for level, b in enumerate(back)]
    half = add(keep, received).reshape(NYL * NZ, 32, 256)
    groups = [[2 * i + c for i in range(NYL * NZ)] for c in range(2)]
    part = lax.all_to_all(half, "tm", 0, 0, axis_index_groups=groups)
    weight_grad = total(part)
    dk, dv = finish(block_pick, own_k, own_v, back)
    return dq, dk, dv, weight_grad


def solution(mesh):
    placed = (P("tm", "head"),) * 5 + (P(None, "head"), P("tm", None))
    return jax.shard_map(
        on_device,
        mesh=mesh,
        in_specs=placed,
        out_specs=(P("tm", "head"),) * 4,
        check_vma=False,
    )
```

```python
import jax
import jax.numpy as jnp
from jax import lax
from jax.experimental import pallas as pl
from jax.experimental.pallas import tpu as pltpu
from jax.sharding import PartitionSpec as P

HD = 128
WIN = 256
BLK = 128
LEVELS = 5
FINISH_MIB = 16
GATE_MIB = 16
ATTEND_MIB = 60
BF = jnp.bfloat16
F32 = jnp.float32
NX, NZ, NYL = 4, 8, 4
VMEM = pl.BlockSpec(memory_space=pltpu.VMEM)
PIECES = 1
ANY = pl.BlockSpec(memory_space=pl.ANY)
SMEM = pl.BlockSpec(memory_space=pltpu.SMEM)


def params(mib=16):
    return pltpu.CompilerParams(vmem_limit_bytes=mib * 1024 * 1024)


def dot(a, b, ca, cb):
    return lax.dot_general(a, b, (((ca,), (cb,)), ((), ())), preferred_element_type=F32)


def pack_kernel(pick, k_ref, v_ref, near_ref, *far_refs):
    near_ref[0:WIN, :] = k_ref[512 - WIN :, :]
    near_ref[WIN : 2 * WIN, :] = v_ref[512 - WIN :, :]
    for level in range(LEVELS):
        first = pl.multiple_of(pick[0, level] * BLK, BLK)
        ref, at = (near_ref, 2 * WIN) if level == 0 else (far_refs[level - 1], 0)
        ref[at : at + BLK, :] = k_ref[pl.ds(first, BLK), :]
        ref[at + BLK : at + 2 * BLK, :] = v_ref[pl.ds(first, BLK), :]


def pack(pick, keys, values):
    return pl.pallas_call(
        pack_kernel,
        out_shape=[jax.ShapeDtypeStruct((2 * WIN + 2 * BLK, 256), BF)]
        + [jax.ShapeDtypeStruct((2 * BLK, 256), BF)] * (LEVELS - 1),
        in_specs=[SMEM, VMEM, VMEM],
        out_specs=[VMEM] * LEVELS,
        compiler_params=params(),
        name="pack",
    )(pick, keys, values)


def k_rows(near_ref, fars, lanes):
    return jnp.concatenate(
        [near_ref[2 * WIN : 2 * WIN + BLK, lanes]] + [r[0:BLK, lanes] for r in fars], axis=0
    )


def v_rows(near_ref, fars, lanes):
    return jnp.concatenate(
        [near_ref[2 * WIN + BLK :, lanes]] + [r[BLK:, lanes] for r in fars], axis=0
    )


def earlier_tile():
    row = lax.broadcasted_iota(jnp.int32, (256, 256), 0)
    col = lax.broadcasted_iota(jnp.int32, (256, 256), 1)
    return row > col


def sources():
    head = lax.axis_index("head")
    yh = head // NX
    return [(yh if at < NX else 1 - yh) * NX + at % NX for at in range(2 * NX)]


def piece(refs, at):
    low = at // NX * 512
    return refs[0][at % NX, low : low + 512, :]


def gate_kernel(*refs):
    refs[-1][...] = jnp.zeros((8, 128), F32)


def gate(*got):
    return pl.pallas_call(
        gate_kernel,
        out_shape=jax.ShapeDtypeStruct((8, 128), F32),
        in_specs=[ANY] * len(got),
        out_specs=VMEM,
        compiler_params=params(GATE_MIB),
        cost_estimate=pl.CostEstimate(
            flops=13000000000, bytes_accessed=2**20, transcendentals=0
        ),
        name="gate",
    )(*got)


def project_kernel(*refs):
    pieces, (w_ref, o_ref, ready) = refs[:PIECES], refs[PIECES : PIECES + 3]
    dout_ref, keep_ref, send_ref = refs[PIECES + 3 :]
    core = lax.axis_index("tm") % 2
    o = o_ref[...]
    acc = jnp.zeros((512, 256), F32)
    for at, src in enumerate(sources()):
        cot = piece(pieces, at)
        acc = acc + dot(cot, w_ref[pl.ds(pl.multiple_of(src * 256, 256), 256), :], 1, 0)
        term = dot(cot, o, 0, 0).astype(BF)
        for sub in range(4):
            rows = pl.ds(pl.multiple_of(src * 128 + sub * 32, 32), 32)
            low = term[sub * 64 : sub * 64 + 32, :]
            high = term[sub * 64 + 32 : sub * 64 + 64, :]
            keep_ref[rows, :] = jnp.where(core == 0, low, high)
            send_ref[rows, :] = jnp.where(core == 0, high, low)
    dout_ref[...] = acc.astype(BF)


def project(pieces, out_weight, outputs, ready):
    half = jax.ShapeDtypeStruct((1024, 256), BF)
    return pl.pallas_call(
        project_kernel,
        out_shape=[jax.ShapeDtypeStruct((512, 256), BF), half, half],
        in_specs=[VMEM] * (PIECES + 2) + [ANY],
        out_specs=[VMEM] * 3,
        compiler_params=params(),
        name="project",
    )(*pieces, out_weight, outputs, ready)


def attend_kernel(
    q_hbm, k_hbm, v_hbm, o_hbm, do_hbm, near_hbm, f1, f2, f3, f4,
    dq_ref, own_ref, back_near, b1, b2, b3, b4, token,
    q_ref, k_ref, v_ref, o_ref, do_ref, near_ref, f_ref, fk, fv, sems,
):
    token[...] = jnp.zeros((8, 128), F32)
    own_k, own_v = own_ref.at[0:512], own_ref.at[512:1024]
    pairs = [(q_hbm, q_ref), (k_hbm, k_ref), (near_hbm, near_ref)]
    pairs += [(f, f_ref.at[i]) for i, f in enumerate((f1, f2, f3, f4))]
    pairs += [(v_hbm, v_ref), (do_hbm, do_ref), (o_hbm, o_ref)]
    loads = [pltpu.make_async_copy(src, dst, sems.at[i]) for i, (src, dst) in enumerate(pairs)]
    for load in loads:
        load.start()
    scale = HD ** (-0.5)
    shard = lax.axis_index("tm")
    neg = jnp.float32(-1e30)
    zero = jnp.zeros((), F32)
    earlier = earlier_tile()
    level_of = lax.broadcasted_iota(jnp.int32, (LEVELS * BLK, 256), 0) // BLK
    far_ok = shard >= (1 << level_of)
    fars = [f_ref.at[i] for i in range(LEVELS - 1)]
    for load in loads[: LEVELS + 2]:
        load.wait()
    for head in range(2):
        lanes = slice(head * HD, (head + 1) * HD)
        k_far = k_rows(near_ref, fars, lanes)
        v_far = v_rows(near_ref, fars, lanes)
        for blk in range(2):
            rows = slice(blk * 256, (blk + 1) * 256)
            q = q_ref[rows, lanes]
            k_here = k_ref[rows, lanes]
            k_prev = near_ref[0:WIN, lanes] if blk == 0 else k_ref[0:256, lanes]
            s_prev = dot(k_prev, q, 1, 1) * scale
            s_here = dot(k_here, q, 1, 1) * scale
            s_far = dot(k_far, q, 1, 1) * scale
            if blk == 0:
                s_prev = jnp.where(shard > 0, s_prev, neg)
            s_near = jnp.where(earlier, s_prev, s_here)
            s_far = jnp.where(far_ok, s_far, neg)
            top = jnp.maximum(
                jnp.max(s_near, axis=0, keepdims=True), jnp.max(s_far, axis=0, keepdims=True)
            )
            e_near, e_far = jnp.exp(s_near - top), jnp.exp(s_far - top)
            inv = 1.0 / (
                jnp.sum(e_near, axis=0, keepdims=True) + jnp.sum(e_far, axis=0, keepdims=True)
            )
            p_near, p_far = e_near * inv, e_far * inv
            if head == 0 and blk == 0:
                for load in loads[LEVELS + 2 :]:
                    load.wait()
            do = do_ref[rows, lanes]
            v_here = v_ref[rows, lanes]
            v_prev = near_ref[WIN : 2 * WIN, lanes] if blk == 0 else v_ref[0:256, lanes]
            delta = jnp.sum(
                do.astype(F32) * o_ref[rows, lanes].astype(F32), axis=1, keepdims=True
            )
            delta = jnp.transpose(jnp.broadcast_to(delta, (256, 128)))[0:1, :]
            dp_near = jnp.where(earlier, dot(v_prev, do, 1, 1), dot(v_here, do, 1, 1))
            dp_far = dot(v_far, do, 1, 1)
            ds_near = p_near * (dp_near - delta)
            ds_far = (p_far * (dp_far - delta)).astype(BF)
            ds_prev = jnp.where(earlier, ds_near, zero).astype(BF)
            ds_here = jnp.where(earlier, zero, ds_near).astype(BF)
            p_prev = jnp.where(earlier, p_near, zero).astype(BF)
            p_here = jnp.where(earlier, zero, p_near).astype(BF)
            p_far = p_far.astype(BF)
            dq = dot(ds_prev, k_prev, 0, 0) + dot(ds_here, k_here, 0, 0) + dot(ds_far, k_far, 0, 0)
            dq_ref[rows, lanes] = (dq * scale).astype(BF)
            dk_prev, dv_prev = dot(ds_prev, q, 1, 0) * scale, dot(p_prev, do, 1, 0)
            dk_here, dv_here = dot(ds_here, q, 1, 0) * scale, dot(p_here, do, 1, 0)
            dk_far, dv_far = dot(ds_far, q, 1, 0) * scale, dot(p_far, do, 1, 0)
            if blk == 0:
                back_near[0:WIN, lanes] = dk_prev.astype(BF)
                back_near[WIN : 2 * WIN, lanes] = dv_prev.astype(BF)
                own_k[0:256, lanes] = dk_here
                own_v[0:256, lanes] = dv_here
                fk[...] = dk_far
                fv[...] = dv_far
            else:
                own_k[0:256, lanes] += dk_prev
                own_v[0:256, lanes] += dv_prev
                own_k[256:512, lanes] = dk_here
                own_v[256:512, lanes] = dv_here
                for i, r in enumerate((back_near, b1, b2, b3, b4)):
                    at = 2 * WIN if i == 0 else 0
                    part = slice(i * BLK, (i + 1) * BLK)
                    r[at : at + BLK, lanes] = (fk[part, :] + dk_far[part]).astype(BF)
                    r[at + BLK : at + 2 * BLK, lanes] = (fv[part, :] + dv_far[part]).astype(BF)


def attend(queries, keys, values, outputs, d_out, got):
    own = jax.ShapeDtypeStruct((1024, 256), F32)
    far = jax.ShapeDtypeStruct((2 * BLK, 256), BF)
    here = pltpu.VMEM((512, 256), BF)
    return pl.pallas_call(
        attend_kernel,
        out_shape=[
            jax.ShapeDtypeStruct((512, 256), BF), own,
            jax.ShapeDtypeStruct((2 * WIN + 2 * BLK, 256), BF), far, far, far, far,
            jax.ShapeDtypeStruct((8, 128), F32),
        ],
        in_specs=[ANY] * 10,
        out_specs=[VMEM] * 8,
        scratch_shapes=[
            here, here, here, here, here,
            pltpu.VMEM((2 * WIN + 2 * BLK, 256), BF),
            pltpu.VMEM((LEVELS - 1, 2 * BLK, 256), BF),
            pltpu.VMEM((LEVELS * BLK, HD), F32),
            pltpu.VMEM((LEVELS * BLK, HD), F32),
            pltpu.SemaphoreType.DMA((10,)),
        ],
        compiler_params=params(ATTEND_MIB),
        name="attend",
    )(queries, keys, values, outputs, d_out, *got)


def add_kernel(keep_ref, got_ref, out_ref):
    out_ref[...] = (keep_ref[...].astype(F32) + got_ref[...].astype(F32)).astype(BF)


def add(keep, received):
    return pl.pallas_call(
        add_kernel,
        out_shape=jax.ShapeDtypeStruct((1024, 256), BF),
        in_specs=[VMEM, VMEM],
        out_specs=VMEM,
        compiler_params=params(),
        name="add",
    )(keep, received)


def total_kernel(part_ref, out_ref):
    out_ref[...] = jnp.sum(part_ref[...].astype(F32), axis=0) * (512 * 64) ** (-0.5)


def total(part):
    return pl.pallas_call(
        total_kernel,
        out_shape=jax.ShapeDtypeStruct((32, 256), F32),
        in_specs=[VMEM],
        out_specs=VMEM,
        compiler_params=params(),
        name="total",
    )(part)


def finish_kernel(pick, own_ref, near_ref, f3, f2, f4, f1, dk_ref, dv_ref, acc):
    for at, out_ref in ((0, dk_ref), (1, dv_ref)):
        acc[0:256, :] = own_ref[at * 512 : at * 512 + 256, :]
        acc[256:512, :] = own_ref[at * 512 + 256 : at * 512 + 512, :] + near_ref[
            at * WIN : (at + 1) * WIN, :
        ].astype(F32)
        for level, far in enumerate((near_ref, f1, f2, f3, f4)):
            low = (2 * WIN if level == 0 else 0) + at * BLK
            rows = pl.ds(pl.multiple_of(pick[0, level] * BLK, BLK), BLK)
            acc[rows, :] += far[low : low + BLK, :].astype(F32)
        out_ref[...] = acc[...].astype(BF)


def finish(pick, own, got):
    out = jax.ShapeDtypeStruct((512, 256), BF)
    return pl.pallas_call(
        finish_kernel,
        out_shape=[out, out],
        in_specs=[SMEM] + [VMEM] * 6,
        out_specs=[VMEM] * 2,
        scratch_shapes=[pltpu.VMEM((512, 256), F32)],
        compiler_params=params(FINISH_MIB),
        cost_estimate=pl.CostEstimate(
            flops=5000000000, bytes_accessed=2**20, transcendentals=0
        ),
        name="finish",
    )(pick, own, got[0], got[3], got[2], got[4], got[1])


def shift(block, distance):
    return lax.ppermute(
        block, "tm", [(i, i + distance) for i in range(64) if 0 <= i + distance < 64]
    )


def spread_kernel(a_ref, b_ref, out_ref):
    for i in range(NX):
        out_ref[i, 0:512, :] = a_ref[...]
        out_ref[i, 512:1024, :] = b_ref[...]


def spread(block, other):
    return pl.pallas_call(
        spread_kernel,
        out_shape=jax.ShapeDtypeStruct((NX, 1024, 256), BF),
        in_specs=[VMEM] * 2,
        out_specs=VMEM,
        compiler_params=params(),
        name="spread",
    )(block, other)


def to_row(blocks):
    rows = [[yh * NX + x for x in range(NX)] for yh in range(2)]
    return lax.all_to_all(blocks, "head", 0, 0, axis_index_groups=rows)


def on_device(queries, keys, values, outputs, out_cotangent, out_weight, block_pick):
    other = lax.ppermute(out_cotangent, "head", [(h, (h + NX) % (2 * NX)) for h in range(2 * NX)])
    packed = pack(block_pick, keys, values)
    got = [shift(b, 2**level) for level, b in enumerate(packed)]
    pieces = [to_row(spread(out_cotangent, other))]
    ready = gate(got[0], got[3], got[2], got[4], got[1])
    d_out, keep, send = project(pieces, out_weight, outputs, ready)
    received = lax.ppermute(send, "tm", [(i, i ^ 1) for i in range(64)])
    dq, own, *back, token = attend(queries, keys, values, outputs, d_out, got)
    back = [shift(b, -(2**level)) for level, b in enumerate(back)]
    half = add(keep, received).reshape(NYL * NZ, 32, 256)
    groups = [[2 * i + c for i in range(NYL * NZ)] for c in range(2)]
    part = lax.all_to_all(half, "tm", 0, 0, axis_index_groups=groups)
    weight_grad = total(part)
    dk, dv = finish(block_pick, own, back)
    return dq, dk, dv, weight_grad


def solution(mesh):
    placed = (P("tm", "head"),) * 5 + (P(None, "head"), P("tm", None))
    return jax.shard_map(
        on_device,
        mesh=mesh,
        in_specs=placed,
        out_specs=(P("tm", "head"),) * 4,
        check_vma=False,
    )
```

```python
import jax
import jax.numpy as jnp
from jax import lax
from jax.experimental import pallas as pl
from jax.experimental.pallas import tpu as pltpu
from jax.sharding import PartitionSpec as P

HD = 128
WIN = 256
BLK = 128
LEVELS = 5
FINISH_MIB = 16
GATE_MIB = 16
ATTEND_MIB = 60
BF = jnp.bfloat16
F32 = jnp.float32
NX, NZ, NYL = 4, 8, 4
VMEM = pl.BlockSpec(memory_space=pltpu.VMEM)
PIECES = 1
ANY = pl.BlockSpec(memory_space=pl.ANY)
SMEM = pl.BlockSpec(memory_space=pltpu.SMEM)


def params(mib=16):
    return pltpu.CompilerParams(vmem_limit_bytes=mib * 1024 * 1024)


def dot(a, b, ca, cb):
    return lax.dot_general(a, b, (((ca,), (cb,)), ((), ())), preferred_element_type=F32)


def pack_kernel(pick, k_ref, v_ref, near_ref, *far_refs):
    near_ref[0:WIN, :] = k_ref[512 - WIN :, :]
    near_ref[WIN : 2 * WIN, :] = v_ref[512 - WIN :, :]
    for level in range(LEVELS):
        first = pl.multiple_of(pick[0, level] * BLK, BLK)
        ref, at = (near_ref, 2 * WIN) if level == 0 else (far_refs[level - 1], 0)
        ref[at : at + BLK, :] = k_ref[pl.ds(first, BLK), :]
        ref[at + BLK : at + 2 * BLK, :] = v_ref[pl.ds(first, BLK), :]


def pack(pick, keys, values):
    return pl.pallas_call(
        pack_kernel,
        out_shape=[jax.ShapeDtypeStruct((2 * WIN + 2 * BLK, 256), BF)]
        + [jax.ShapeDtypeStruct((2 * BLK, 256), BF)] * (LEVELS - 1),
        in_specs=[SMEM, VMEM, VMEM],
        out_specs=[VMEM] * LEVELS,
        compiler_params=params(),
        name="pack",
    )(pick, keys, values)


def k_rows(near_ref, fars, lanes):
    return jnp.concatenate(
        [near_ref[2 * WIN : 2 * WIN + BLK, lanes]] + [r[0:BLK, lanes] for r in fars], axis=0
    )


def v_rows(near_ref, fars, lanes):
    return jnp.concatenate(
        [near_ref[2 * WIN + BLK :, lanes]] + [r[BLK:, lanes] for r in fars], axis=0
    )


def earlier_tile():
    row = lax.broadcasted_iota(jnp.int32, (256, 256), 0)
    col = lax.broadcasted_iota(jnp.int32, (256, 256), 1)
    return row > col


def sources():
    head = lax.axis_index("head")
    yh = head // NX
    return [(yh if at < NX else 1 - yh) * NX + at % NX for at in range(2 * NX)]


def piece(refs, at):
    low = at // NX * 512
    return refs[0][at % NX, low : low + 512, :]


def gate_kernel(*refs):
    refs[-1][...] = jnp.zeros((8, 128), F32)


def gate(*got):
    return pl.pallas_call(
        gate_kernel,
        out_shape=jax.ShapeDtypeStruct((8, 128), F32),
        in_specs=[ANY] * len(got),
        out_specs=VMEM,
        compiler_params=params(GATE_MIB),
        cost_estimate=pl.CostEstimate(
            flops=13000000000, bytes_accessed=2**20, transcendentals=0
        ),
        name="gate",
    )(*got)


def project_kernel(*refs):
    pieces, (w_ref, o_ref, ready) = refs[:PIECES], refs[PIECES : PIECES + 3]
    dout_ref, keep_ref, send_ref = refs[PIECES + 3 :]
    core = lax.axis_index("tm") % 2
    o = o_ref[...]
    acc = jnp.zeros((512, 256), F32)
    for at, src in enumerate(sources()):
        cot = piece(pieces, at)
        acc = acc + dot(cot, w_ref[pl.ds(pl.multiple_of(src * 256, 256), 256), :], 1, 0)
        term = dot(cot, o, 0, 0).astype(BF)
        for sub in range(4):
            rows = pl.ds(pl.multiple_of((src % 2 * 4 + sub) * 128 + src // 2 * 32, 32), 32)
            low = term[sub * 64 : sub * 64 + 32, :]
            high = term[sub * 64 + 32 : sub * 64 + 64, :]
            keep_ref[rows, :] = jnp.where(core == 0, low, high)
            send_ref[rows, :] = jnp.where(core == 0, high, low)
    dout_ref[...] = acc.astype(BF)


def project(pieces, out_weight, outputs, ready):
    half = jax.ShapeDtypeStruct((1024, 256), BF)
    return pl.pallas_call(
        project_kernel,
        out_shape=[jax.ShapeDtypeStruct((512, 256), BF), half, half],
        in_specs=[VMEM] * (PIECES + 2) + [ANY],
        out_specs=[VMEM] * 3,
        compiler_params=params(),
        name="project",
    )(*pieces, out_weight, outputs, ready)


def attend_kernel(
    q_hbm, k_hbm, v_hbm, o_hbm, do_hbm, near_hbm, f1, f2, f3, f4,
    dq_ref, own_ref, back_near, b1, b2, b3, b4, token,
    q_ref, k_ref, v_ref, o_ref, do_ref, near_ref, f_ref, fk, fv, sems,
):
    token[...] = jnp.zeros((8, 128), F32)
    own_k, own_v = own_ref.at[0:512], own_ref.at[512:1024]
    pairs = [(q_hbm, q_ref), (k_hbm, k_ref), (near_hbm, near_ref)]
    pairs += [(f, f_ref.at[i]) for i, f in enumerate((f1, f2, f3, f4))]
    pairs += [(v_hbm, v_ref), (do_hbm, do_ref), (o_hbm, o_ref)]
    loads = [pltpu.make_async_copy(src, dst, sems.at[i]) for i, (src, dst) in enumerate(pairs)]
    for load in loads:
        load.start()
    scale = HD ** (-0.5)
    shard = lax.axis_index("tm")
    neg = jnp.float32(-1e30)
    zero = jnp.zeros((), F32)
    earlier = earlier_tile()
    level_of = lax.broadcasted_iota(jnp.int32, (LEVELS * BLK, 256), 0) // BLK
    far_ok = shard >= (1 << level_of)
    fars = [f_ref.at[i] for i in range(LEVELS - 1)]
    for load in loads[: LEVELS + 2]:
        load.wait()
    for head in range(2):
        lanes = slice(head * HD, (head + 1) * HD)
        k_far = k_rows(near_ref, fars, lanes)
        v_far = v_rows(near_ref, fars, lanes)
        for blk in range(2):
            rows = slice(blk * 256, (blk + 1) * 256)
            q = q_ref[rows, lanes]
            k_here = k_ref[rows, lanes]
            k_prev = near_ref[0:WIN, lanes] if blk == 0 else k_ref[0:256, lanes]
            s_prev = dot(k_prev, q, 1, 1) * scale
            s_here = dot(k_here, q, 1, 1) * scale
            s_far = dot(k_far, q, 1, 1) * scale
            if blk == 0:
                s_prev = jnp.where(shard > 0, s_prev, neg)
            s_near = jnp.where(earlier, s_prev, s_here)
            s_far = jnp.where(far_ok, s_far, neg)
            top = jnp.maximum(
                jnp.max(s_near, axis=0, keepdims=True), jnp.max(s_far, axis=0, keepdims=True)
            )
            e_near, e_far = jnp.exp(s_near - top), jnp.exp(s_far - top)
            inv = 1.0 / (
                jnp.sum(e_near, axis=0, keepdims=True) + jnp.sum(e_far, axis=0, keepdims=True)
            )
            p_near, p_far = e_near * inv, e_far * inv
            if head == 0 and blk == 0:
                for load in loads[LEVELS + 2 :]:
                    load.wait()
            do = do_ref[rows, lanes]
            v_here = v_ref[rows, lanes]
            v_prev = near_ref[WIN : 2 * WIN, lanes] if blk == 0 else v_ref[0:256, lanes]
            delta = jnp.sum(
                do.astype(F32) * o_ref[rows, lanes].astype(F32), axis=1, keepdims=True
            )
            delta = jnp.transpose(jnp.broadcast_to(delta, (256, 128)))[0:1, :]
            dp_near = jnp.where(earlier, dot(v_prev, do, 1, 1), dot(v_here, do, 1, 1))
            dp_far = dot(v_far, do, 1, 1)
            ds_near = p_near * (dp_near - delta)
            ds_far = (p_far * (dp_far - delta)).astype(BF)
            ds_prev = jnp.where(earlier, ds_near, zero).astype(BF)
            ds_here = jnp.where(earlier, zero, ds_near).astype(BF)
            p_prev = jnp.where(earlier, p_near, zero).astype(BF)
            p_here = jnp.where(earlier, zero, p_near).astype(BF)
            p_far = p_far.astype(BF)
            dq = dot(ds_prev, k_prev, 0, 0) + dot(ds_here, k_here, 0, 0) + dot(ds_far, k_far, 0, 0)
            dq_ref[rows, lanes] = (dq * scale).astype(BF)
            dk_prev, dv_prev = dot(ds_prev, q, 1, 0) * scale, dot(p_prev, do, 1, 0)
            dk_here, dv_here = dot(ds_here, q, 1, 0) * scale, dot(p_here, do, 1, 0)
            dk_far, dv_far = dot(ds_far, q, 1, 0) * scale, dot(p_far, do, 1, 0)
            if blk == 0:
                back_near[0:WIN, lanes] = dk_prev.astype(BF)
                back_near[WIN : 2 * WIN, lanes] = dv_prev.astype(BF)
                own_k[0:256, lanes] = dk_here
                own_v[0:256, lanes] = dv_here
                fk[...] = dk_far
                fv[...] = dv_far
            else:
                own_k[0:256, lanes] += dk_prev
                own_v[0:256, lanes] += dv_prev
                own_k[256:512, lanes] = dk_here
                own_v[256:512, lanes] = dv_here
                for i, r in enumerate((back_near, b1, b2, b3, b4)):
                    at = 2 * WIN if i == 0 else 0
                    part = slice(i * BLK, (i + 1) * BLK)
                    r[at : at + BLK, lanes] = (fk[part, :] + dk_far[part]).astype(BF)
                    r[at + BLK : at + 2 * BLK, lanes] = (fv[part, :] + dv_far[part]).astype(BF)


def attend(queries, keys, values, outputs, d_out, got):
    own = jax.ShapeDtypeStruct((1024, 256), F32)
    far = jax.ShapeDtypeStruct((2 * BLK, 256), BF)
    here = pltpu.VMEM((512, 256), BF)
    return pl.pallas_call(
        attend_kernel,
        out_shape=[
            jax.ShapeDtypeStruct((512, 256), BF), own,
            jax.ShapeDtypeStruct((2 * WIN + 2 * BLK, 256), BF), far, far, far, far,
            jax.ShapeDtypeStruct((8, 128), F32),
        ],
        in_specs=[ANY] * 10,
        out_specs=[VMEM] * 8,
        scratch_shapes=[
            here, here, here, here, here,
            pltpu.VMEM((2 * WIN + 2 * BLK, 256), BF),
            pltpu.VMEM((LEVELS - 1, 2 * BLK, 256), BF),
            pltpu.VMEM((LEVELS * BLK, HD), F32),
            pltpu.VMEM((LEVELS * BLK, HD), F32),
            pltpu.SemaphoreType.DMA((10,)),
        ],
        compiler_params=params(ATTEND_MIB),
        name="attend",
    )(queries, keys, values, outputs, d_out, *got)


def add_kernel(keep_ref, got_ref, out_ref):
    out_ref[...] = (keep_ref[...].astype(F32) + got_ref[...].astype(F32)).astype(BF)


def add(keep, received):
    return pl.pallas_call(
        add_kernel,
        out_shape=jax.ShapeDtypeStruct((1024, 256), BF),
        in_specs=[VMEM, VMEM],
        out_specs=VMEM,
        compiler_params=params(),
        name="add",
    )(keep, received)


def part_kernel(half_ref, out_ref):
    out_ref[...] = jnp.sum(half_ref[...].astype(F32), axis=0).astype(BF)


def part_sum(half):
    return pl.pallas_call(
        part_kernel,
        out_shape=jax.ShapeDtypeStruct((NYL, 32, 256), BF),
        in_specs=[VMEM],
        out_specs=VMEM,
        compiler_params=params(),
        name="part_sum",
    )(half)


def total_kernel(part_ref, out_ref):
    out_ref[...] = jnp.sum(part_ref[...].astype(F32), axis=0) * (512 * 64) ** (-0.5)


def total(part):
    return pl.pallas_call(
        total_kernel,
        out_shape=jax.ShapeDtypeStruct((32, 256), F32),
        in_specs=[VMEM],
        out_specs=VMEM,
        compiler_params=params(),
        name="total",
    )(part)


def finish_kernel(pick, own_ref, near_ref, f3, f2, f4, f1, dk_ref, dv_ref, acc):
    for at, out_ref in ((0, dk_ref), (1, dv_ref)):
        acc[0:256, :] = own_ref[at * 512 : at * 512 + 256, :]
        acc[256:512, :] = own_ref[at * 512 + 256 : at * 512 + 512, :] + near_ref[
            at * WIN : (at + 1) * WIN, :
        ].astype(F32)
        for level, far in enumerate((near_ref, f1, f2, f3, f4)):
            low = (2 * WIN if level == 0 else 0) + at * BLK
            rows = pl.ds(pl.multiple_of(pick[0, level] * BLK, BLK), BLK)
            acc[rows, :] += far[low : low + BLK, :].astype(F32)
        out_ref[...] = acc[...].astype(BF)


def finish(pick, own, got):
    out = jax.ShapeDtypeStruct((512, 256), BF)
    return pl.pallas_call(
        finish_kernel,
        out_shape=[out, out],
        in_specs=[SMEM] + [VMEM] * 6,
        out_specs=[VMEM] * 2,
        scratch_shapes=[pltpu.VMEM((512, 256), F32)],
        compiler_params=params(FINISH_MIB),
        cost_estimate=pl.CostEstimate(
            flops=5000000000, bytes_accessed=2**20, transcendentals=0
        ),
        name="finish",
    )(pick, own, got[0], got[3], got[2], got[4], got[1])


def shift(block, distance):
    return lax.ppermute(
        block, "tm", [(i, i + distance) for i in range(64) if 0 <= i + distance < 64]
    )


def spread_kernel(a_ref, b_ref, out_ref):
    for i in range(NX):
        out_ref[i, 0:512, :] = a_ref[...]
        out_ref[i, 512:1024, :] = b_ref[...]


def spread(block, other):
    return pl.pallas_call(
        spread_kernel,
        out_shape=jax.ShapeDtypeStruct((NX, 1024, 256), BF),
        in_specs=[VMEM] * 2,
        out_specs=VMEM,
        compiler_params=params(),
        name="spread",
    )(block, other)


def to_row(blocks):
    rows = [[yh * NX + x for x in range(NX)] for yh in range(2)]
    return lax.all_to_all(blocks, "head", 0, 0, axis_index_groups=rows)


def on_device(queries, keys, values, outputs, out_cotangent, out_weight, block_pick):
    other = lax.ppermute(out_cotangent, "head", [(h, (h + NX) % (2 * NX)) for h in range(2 * NX)])
    packed = pack(block_pick, keys, values)
    got = [shift(b, 2**level) for level, b in enumerate(packed)]
    pieces = [to_row(spread(out_cotangent, other))]
    ready = gate(got[0], got[3], got[2], got[4], got[1])
    d_out, keep, send = project(pieces, out_weight, outputs, ready)
    received = lax.ppermute(send, "tm", [(i, i ^ 1) for i in range(64)])
    dq, own, *back, token = attend(queries, keys, values, outputs, d_out, got)
    back = [shift(b, -(2**level)) for level, b in enumerate(back)]
    half = add(keep, received).reshape(NZ, NYL, 32, 256)
    z_groups = [[yl * 16 + z * 2 + c for z in range(NZ)] for yl in range(NYL) for c in range(2)]
    half = lax.all_to_all(half, "tm", 0, 0, axis_index_groups=z_groups)
    y_groups = [[yl * 16 + zc for yl in range(NYL)] for zc in range(16)]
    part = lax.all_to_all(part_sum(half), "tm", 0, 0, axis_index_groups=y_groups)
    weight_grad = total(part)
    dk, dv = finish(block_pick, own, back)
    return dq, dk, dv, weight_grad


def solution(mesh):
    placed = (P("tm", "head"),) * 5 + (P(None, "head"), P("tm", None))
    return jax.shard_map(
        on_device,
        mesh=mesh,
        in_specs=placed,
        out_specs=(P("tm", "head"),) * 4,
        check_vma=False,
    )
```

```python
import jax
import jax.numpy as jnp
from jax import lax
from jax.experimental import pallas as pl
from jax.experimental.pallas import tpu as pltpu
from jax.sharding import PartitionSpec as P

HD = 128
WIN = 256
BLK = 128
LEVELS = 5
FINISH_MIB = 16
GATE_MIB = 60
ATTEND_MIB = 60
BF = jnp.bfloat16
F32 = jnp.float32
NX, NZ, NYL = 4, 8, 4
VMEM = pl.BlockSpec(memory_space=pltpu.VMEM)
PIECES = 1
ANY = pl.BlockSpec(memory_space=pl.ANY)
SMEM = pl.BlockSpec(memory_space=pltpu.SMEM)


def params(mib=16):
    return pltpu.CompilerParams(vmem_limit_bytes=mib * 1024 * 1024)


def dot(a, b, ca, cb):
    return lax.dot_general(a, b, (((ca,), (cb,)), ((), ())), preferred_element_type=F32)


def pack_kernel(pick, k_ref, v_ref, near_ref, *far_refs):
    near_ref[0:WIN, :] = k_ref[512 - WIN :, :]
    near_ref[WIN : 2 * WIN, :] = v_ref[512 - WIN :, :]
    for level in range(LEVELS):
        first = pl.multiple_of(pick[0, level] * BLK, BLK)
        ref, at = (near_ref, 2 * WIN) if level == 0 else (far_refs[level - 1], 0)
        ref[at : at + BLK, :] = k_ref[pl.ds(first, BLK), :]
        ref[at + BLK : at + 2 * BLK, :] = v_ref[pl.ds(first, BLK), :]


def pack(pick, keys, values):
    return pl.pallas_call(
        pack_kernel,
        out_shape=[jax.ShapeDtypeStruct((2 * WIN + 2 * BLK, 256), BF)]
        + [jax.ShapeDtypeStruct((2 * BLK, 256), BF)] * (LEVELS - 1),
        in_specs=[SMEM, VMEM, VMEM],
        out_specs=[VMEM] * LEVELS,
        compiler_params=params(),
        name="pack",
    )(pick, keys, values)


def k_rows(near_ref, fars, lanes):
    return jnp.concatenate(
        [near_ref[2 * WIN : 2 * WIN + BLK, lanes]] + [r[0:BLK, lanes] for r in fars], axis=0
    )


def v_rows(near_ref, fars, lanes):
    return jnp.concatenate(
        [near_ref[2 * WIN + BLK :, lanes]] + [r[BLK:, lanes] for r in fars], axis=0
    )


def earlier_tile():
    row = lax.broadcasted_iota(jnp.int32, (256, 256), 0)
    col = lax.broadcasted_iota(jnp.int32, (256, 256), 1)
    return row > col


def sources():
    head = lax.axis_index("head")
    yh = head // NX
    return [(yh if at < NX else 1 - yh) * NX + at % NX for at in range(2 * NX)]


def piece(refs, at):
    low = at // NX * 512
    return refs[0][at % NX, low : low + 512, :]


def gate_kernel(*refs):
    refs[-1][0, 0] = jnp.int32(0)


def gate(*got):
    return pl.pallas_call(
        gate_kernel,
        out_shape=jax.ShapeDtypeStruct((1, 128), jnp.int32),
        in_specs=[ANY] * len(got),
        out_specs=SMEM,
        compiler_params=params(GATE_MIB),
        cost_estimate=pl.CostEstimate(
            flops=13000000000, bytes_accessed=2**20, transcendentals=0
        ),
        name="gate",
    )(*got)


def project_kernel(*refs):
    pieces, (w_ref, o_ref, ready) = refs[:PIECES], refs[PIECES : PIECES + 3]
    dout_ref, keep_ref, send_ref = refs[PIECES + 3 :]
    core = lax.axis_index("tm") % 2
    o = o_ref[...]
    acc = jnp.zeros((512, 256), F32)
    for at, src in enumerate(sources()):
        cot = piece(pieces, at)
        acc = acc + dot(cot, w_ref[pl.ds(pl.multiple_of(src * 256, 256), 256), :], 1, 0)
        term = dot(cot, o, 0, 0).astype(BF)
        for sub in range(4):
            rows = pl.ds(pl.multiple_of((src % 2 * 4 + sub) * 128 + src // 2 * 32, 32), 32)
            low = term[sub * 64 : sub * 64 + 32, :]
            high = term[sub * 64 + 32 : sub * 64 + 64, :]
            keep_ref[rows, :] = jnp.where(core == 0, low, high)
            send_ref[rows, :] = jnp.where(core == 0, high, low)
    dout_ref[...] = acc.astype(BF)


def project(pieces, out_weight, outputs, ready):
    half = jax.ShapeDtypeStruct((1024, 256), BF)
    return pl.pallas_call(
        project_kernel,
        out_shape=[jax.ShapeDtypeStruct((512, 256), BF), half, half],
        in_specs=[VMEM] * (PIECES + 2) + [SMEM],
        out_specs=[VMEM] * 3,
        compiler_params=params(),
        name="project",
    )(*pieces, out_weight, outputs, ready)


def attend_kernel(
    q_hbm, k_hbm, v_hbm, o_hbm, do_hbm, near_hbm, f1, f2, f3, f4,
    dq_ref, own_ref, back_near, b1, b2, b3, b4, token,
    q_ref, k_ref, v_ref, o_ref, do_ref, near_ref, f_ref, fk, fv, sems,
):
    token[...] = jnp.zeros((8, 128), F32)
    own_k, own_v = own_ref.at[0:512], own_ref.at[512:1024]
    pairs = [(q_hbm, q_ref), (k_hbm, k_ref), (near_hbm, near_ref)]
    pairs += [(f, f_ref.at[i]) for i, f in enumerate((f1, f2, f3, f4))]
    pairs += [(v_hbm, v_ref), (do_hbm, do_ref), (o_hbm, o_ref)]
    loads = [pltpu.make_async_copy(src, dst, sems.at[i]) for i, (src, dst) in enumerate(pairs)]
    for load in loads:
        load.start()
    scale = HD ** (-0.5)
    shard = lax.axis_index("tm")
    neg = jnp.float32(-1e30)
    zero = jnp.zeros((), F32)
    earlier = earlier_tile()
    level_of = lax.broadcasted_iota(jnp.int32, (LEVELS * BLK, 256), 0) // BLK
    far_ok = shard >= (1 << level_of)
    fars = [f_ref.at[i] for i in range(LEVELS - 1)]
    for load in loads[: LEVELS + 2]:
        load.wait()
    for head in range(2):
        lanes = slice(head * HD, (head + 1) * HD)
        k_far = k_rows(near_ref, fars, lanes)
        v_far = v_rows(near_ref, fars, lanes)
        for blk in range(2):
            rows = slice(blk * 256, (blk + 1) * 256)
            q = q_ref[rows, lanes]
            k_here = k_ref[rows, lanes]
            k_prev = near_ref[0:WIN, lanes] if blk == 0 else k_ref[0:256, lanes]
            s_prev = dot(k_prev, q, 1, 1) * scale
            s_here = dot(k_here, q, 1, 1) * scale
            s_far = dot(k_far, q, 1, 1) * scale
            if blk == 0:
                s_prev = jnp.where(shard > 0, s_prev, neg)
            s_near = jnp.where(earlier, s_prev, s_here)
            s_far = jnp.where(far_ok, s_far, neg)
            top = jnp.maximum(
                jnp.max(s_near, axis=0, keepdims=True), jnp.max(s_far, axis=0, keepdims=True)
            )
            e_near, e_far = jnp.exp(s_near - top), jnp.exp(s_far - top)
            inv = 1.0 / (
                jnp.sum(e_near, axis=0, keepdims=True) + jnp.sum(e_far, axis=0, keepdims=True)
            )
            p_near, p_far = e_near * inv, e_far * inv
            if head == 0 and blk == 0:
                for load in loads[LEVELS + 2 :]:
                    load.wait()
            do = do_ref[rows, lanes]
            v_here = v_ref[rows, lanes]
            v_prev = near_ref[WIN : 2 * WIN, lanes] if blk == 0 else v_ref[0:256, lanes]
            delta = jnp.sum(
                do.astype(F32) * o_ref[rows, lanes].astype(F32), axis=1, keepdims=True
            )
            delta = jnp.transpose(jnp.broadcast_to(delta, (256, 128)))[0:1, :]
            dp_near = jnp.where(earlier, dot(v_prev, do, 1, 1), dot(v_here, do, 1, 1))
            dp_far = dot(v_far, do, 1, 1)
            ds_near = p_near * (dp_near - delta)
            ds_far = (p_far * (dp_far - delta)).astype(BF)
            ds_prev = jnp.where(earlier, ds_near, zero).astype(BF)
            ds_here = jnp.where(earlier, zero, ds_near).astype(BF)
            p_prev = jnp.where(earlier, p_near, zero).astype(BF)
            p_here = jnp.where(earlier, zero, p_near).astype(BF)
            p_far = p_far.astype(BF)
            dq = dot(ds_prev, k_prev, 0, 0) + dot(ds_here, k_here, 0, 0) + dot(ds_far, k_far, 0, 0)
            dq_ref[rows, lanes] = (dq * scale).astype(BF)
            dk_prev, dv_prev = dot(ds_prev, q, 1, 0) * scale, dot(p_prev, do, 1, 0)
            dk_here, dv_here = dot(ds_here, q, 1, 0) * scale, dot(p_here, do, 1, 0)
            dk_far, dv_far = dot(ds_far, q, 1, 0) * scale, dot(p_far, do, 1, 0)
            if blk == 0:
                back_near[0:WIN, lanes] = dk_prev.astype(BF)
                back_near[WIN : 2 * WIN, lanes] = dv_prev.astype(BF)
                own_k[0:256, lanes] = dk_here
                own_v[0:256, lanes] = dv_here
                fk[...] = dk_far
                fv[...] = dv_far
            else:
                own_k[0:256, lanes] += dk_prev
                own_v[0:256, lanes] += dv_prev
                own_k[256:512, lanes] = dk_here
                own_v[256:512, lanes] = dv_here
                for i, r in enumerate((back_near, b1, b2, b3, b4)):
                    at = 2 * WIN if i == 0 else 0
                    part = slice(i * BLK, (i + 1) * BLK)
                    r[at : at + BLK, lanes] = (fk[part, :] + dk_far[part]).astype(BF)
                    r[at + BLK : at + 2 * BLK, lanes] = (fv[part, :] + dv_far[part]).astype(BF)


def attend(queries, keys, values, outputs, d_out, got):
    own = jax.ShapeDtypeStruct((1024, 256), F32)
    far = jax.ShapeDtypeStruct((2 * BLK, 256), BF)
    here = pltpu.VMEM((512, 256), BF)
    return pl.pallas_call(
        attend_kernel,
        out_shape=[
            jax.ShapeDtypeStruct((512, 256), BF), own,
            jax.ShapeDtypeStruct((2 * WIN + 2 * BLK, 256), BF), far, far, far, far,
            jax.ShapeDtypeStruct((8, 128), F32),
        ],
        in_specs=[ANY] * 10,
        out_specs=[VMEM] * 8,
        scratch_shapes=[
            here, here, here, here, here,
            pltpu.VMEM((2 * WIN + 2 * BLK, 256), BF),
            pltpu.VMEM((LEVELS - 1, 2 * BLK, 256), BF),
            pltpu.VMEM((LEVELS * BLK, HD), F32),
            pltpu.VMEM((LEVELS * BLK, HD), F32),
            pltpu.SemaphoreType.DMA((10,)),
        ],
        compiler_params=params(ATTEND_MIB),
        name="attend",
    )(queries, keys, values, outputs, d_out, *got)


def add_kernel(keep_ref, got_ref, out_ref):
    out_ref[...] = (keep_ref[...].astype(F32) + got_ref[...].astype(F32)).astype(BF)


def add(keep, received):
    return pl.pallas_call(
        add_kernel,
        out_shape=jax.ShapeDtypeStruct((1024, 256), BF),
        in_specs=[VMEM, VMEM],
        out_specs=VMEM,
        compiler_params=params(),
        name="add",
    )(keep, received)


def part_kernel(half_ref, out_ref):
    out_ref[...] = jnp.sum(half_ref[...].astype(F32), axis=0).astype(BF)


def part_sum(half):
    return pl.pallas_call(
        part_kernel,
        out_shape=jax.ShapeDtypeStruct((NYL, 32, 256), BF),
        in_specs=[VMEM],
        out_specs=VMEM,
        compiler_params=params(),
        name="part_sum",
    )(half)


def total_kernel(part_ref, out_ref):
    out_ref[...] = jnp.sum(part_ref[...].astype(F32), axis=0) * (512 * 64) ** (-0.5)


def total(part):
    return pl.pallas_call(
        total_kernel,
        out_shape=jax.ShapeDtypeStruct((32, 256), F32),
        in_specs=[VMEM],
        out_specs=VMEM,
        compiler_params=params(),
        name="total",
    )(part)


def finish_kernel(pick, own_ref, near_ref, f3, f2, f4, f1, dk_ref, dv_ref, acc):
    for at, out_ref in ((0, dk_ref), (1, dv_ref)):
        acc[0:256, :] = own_ref[at * 512 : at * 512 + 256, :]
        acc[256:512, :] = own_ref[at * 512 + 256 : at * 512 + 512, :] + near_ref[
            at * WIN : (at + 1) * WIN, :
        ].astype(F32)
        for level, far in enumerate((near_ref, f1, f2, f3, f4)):
            low = (2 * WIN if level == 0 else 0) + at * BLK
            rows = pl.ds(pl.multiple_of(pick[0, level] * BLK, BLK), BLK)
            acc[rows, :] += far[low : low + BLK, :].astype(F32)
        out_ref[...] = acc[...].astype(BF)


def finish(pick, own, got):
    out = jax.ShapeDtypeStruct((512, 256), BF)
    return pl.pallas_call(
        finish_kernel,
        out_shape=[out, out],
        in_specs=[SMEM] + [VMEM] * 6,
        out_specs=[VMEM] * 2,
        scratch_shapes=[pltpu.VMEM((512, 256), F32)],
        compiler_params=params(FINISH_MIB),
        cost_estimate=pl.CostEstimate(
            flops=5000000000, bytes_accessed=2**20, transcendentals=0
        ),
        name="finish",
    )(pick, own, got[0], got[3], got[2], got[4], got[1])


def shift(block, distance):
    return lax.ppermute(
        block, "tm", [(i, i + distance) for i in range(64) if 0 <= i + distance < 64]
    )


def spread_kernel(a_ref, b_ref, out_ref):
    for i in range(NX):
        out_ref[i, 0:512, :] = a_ref[...]
        out_ref[i, 512:1024, :] = b_ref[...]


def spread(block, other):
    return pl.pallas_call(
        spread_kernel,
        out_shape=jax.ShapeDtypeStruct((NX, 1024, 256), BF),
        in_specs=[VMEM] * 2,
        out_specs=VMEM,
        compiler_params=params(),
        name="spread",
    )(block, other)


def to_row(blocks):
    rows = [[yh * NX + x for x in range(NX)] for yh in range(2)]
    return lax.all_to_all(blocks, "head", 0, 0, axis_index_groups=rows)


def on_device(queries, keys, values, outputs, out_cotangent, out_weight, block_pick):
    other = lax.ppermute(out_cotangent, "head", [(h, (h + NX) % (2 * NX)) for h in range(2 * NX)])
    packed = pack(block_pick, keys, values)
    got = [shift(b, 2**level) for level, b in enumerate(packed)]
    pieces = [to_row(spread(out_cotangent, other))]
    ready = gate(got[0], got[3], got[2], got[4], got[1])
    d_out, keep, send = project(pieces, out_weight, outputs, ready)
    received = lax.ppermute(send, "tm", [(i, i ^ 1) for i in range(64)])
    dq, own, *back, token = attend(queries, keys, values, outputs, d_out, got)
    back = [shift(b, -(2**level)) for level, b in enumerate(back)]
    half = add(keep, received).reshape(NZ, NYL, 32, 256)
    z_groups = [[yl * 16 + z * 2 + c for z in range(NZ)] for yl in range(NYL) for c in range(2)]
    half = lax.all_to_all(half, "tm", 0, 0, axis_index_groups=z_groups)
    y_groups = [[yl * 16 + zc for yl in range(NYL)] for zc in range(16)]
    part = lax.all_to_all(part_sum(half), "tm", 0, 0, axis_index_groups=y_groups)
    weight_grad = total(part)
    dk, dv = finish(block_pick, own, back)
    return dq, dk, dv, weight_grad


def solution(mesh):
    placed = (P("tm", "head"),) * 5 + (P(None, "head"), P("tm", None))
    return jax.shard_map(
        on_device,
        mesh=mesh,
        in_specs=placed,
        out_specs=(P("tm", "head"),) * 4,
        check_vma=False,
    )
```
